768 devices in a mesh: gx: 3 (over z_lo), gy: 16 (over y, core), gz: 16 (over z_hi, x).
Axes of the slice: x: 4, y: 8, z: 12 (z_hi: 4, z_lo: 3; z = z_hi * 3 + z_lo), core: 2. Of those that a mesh axis runs over, the one named last changes fastest.
Arguments:
- positions: float32 [3, 16, 16, 3, 18], P('gx', 'gy', 'gz'), may hold values from 0 to 7, as said below
- species: int32 [3, 16, 16, 18], P('gx', 'gy', 'gz'), may hold values from 0 to 88
- send_rows: int32 [3, 16, 16, 18], P('gx', 'gy', 'gz'), may hold values from 0 to 17, as said below
- neighbours: int32 [3, 16, 16, 56, 18], P('gx', 'gy', 'gz'), may hold values from -1 to 503, as said below
- embedding: float32 [89, 128], replicated, may hold values from -6 to 6
- self_energy: float32 [89], replicated, may hold values from -6 to 6
- source_weight: float32 [2, 128, 128], replicated, may hold values from -0.5 to 0.5
- radial_in: float32 [2, 8, 64], replicated, may hold values from -6 to 6
- radial_out: float32 [2, 64, 384], replicated, may hold values from -0.75 to 0.75
- mix_weight: float32 [2, 384, 128], replicated, may hold values from -0.3125 to 0.3125
- read_one: float32 [128], replicated, may hold values from -0.5 to 0.5
- read_hidden: float32 [128, 16], replicated, may hold values from -0.5 to 0.5
- read_two: float32 [16], replicated, may hold values from -1.5 to 1.5
Outputs:
- atom_energy: float32 [3, 16, 16, 18], P('gx', 'gy', 'gz')
- forces: float32 [3, 16, 16, 3, 18], P('gx', 'gy', 'gz')
The draws below stay inside these ranges and needn't reach their ends.
Inputs may be any that keep to these rules, and one draw needn't show every extreme that they name: `positions`: atom a lies within 0.4 of each coordinate of its lattice cell's centre 2.5 (a // 6 + 0.5, a // 2 % 3 + 0.5, a % 2 + 0.5). `send_rows`: the 18 entries of a domain are a permutation of its 18 atoms (with 3 = 3 and 2 = 2 every lattice cell lies in the outer two layers). `neighbours`: entries are rows of the domain's row table of 504 rows; -1 marks an empty slot. No entry names block b = 13 or a domain beyond the ends of gz; every named row lies within 8.5 of the atom, and every atom within 6 of an atom either is named in one of its slots or has been left out of its list.
All inputs are finite; a program needn't handle non-finite values.
Results may differ from the reference program's by a relative error of at most 0.0003.
Values sent between devices are 32-bit elements; how exact they have to be, the bound alone decides.
A program may use at most 32 MiB of HBM per device.

```python
import math
import jax
import jax.numpy as jnp
import numpy as np
from jax import lax

C = 128
SPECIES = 89
NB = 8
RH = 64
RO = 16
LAYERS = 2
K = 56
SIDE = 3
LZ = 2
A = 18
G = 18
N_GX = 3
N_GY = 16
N_GZ = 16


SPACING = 2.5


DELTAS = np.array([[step_x, step_y, step_z] for step_x in range(-2, 3) for step_y in range(-2, 3) for step_z in range(-2, 3) if 0 < step_x * step_x + step_y * step_y + step_z * step_z <= 5], np.int32)


def lattice_coords():
    lattice_ids = jnp.arange(A, dtype=jnp.int32)
    coord_x = lattice_ids // (SIDE * LZ)
    coord_y = lattice_ids // LZ % SIDE
    coord_z = lattice_ids % LZ
    return (lattice_ids, coord_x, coord_y, coord_z)


def shell_order(key):
    lattice_ids, coord_x, coord_y, coord_z = lattice_coords()
    border = (coord_x < 2) | (coord_x >= SIDE - 2) | (coord_y < 2) | (coord_y >= SIDE - 2) | (coord_z < 2) | (coord_z >= LZ - 2)
    scores = jax.random.randint(key, (N_GX, N_GY, N_GZ, A), 0, 2 ** 19)
    ranked = jnp.where(border[None, None, None, :], scores * 2048 + lattice_ids, 2 ** 30 + lattice_ids)
    ranked = jnp.where((lattice_ids == 0)[None, None, None, :], 2 ** 30 - 1, ranked)
    return jnp.argsort(ranked, axis=-1).astype(jnp.int32)


def draw_send_rows(key, part):
    ordered = shell_order(key)
    return ordered[..., :G].astype(jnp.int32)


def draw_neighbours(key, part):
    ordered = shell_order(key)
    key = jax.random.fold_in(key, 7)
    inverse = jnp.argsort(ordered, axis=-1).astype(jnp.int32)
    lattice_ids, coord_x, coord_y, coord_z = lattice_coords()
    deltas = jnp.array(DELTAS, jnp.int32)
    moved_x = coord_x[None, :] + deltas[:, 0:1]
    moved_y = coord_y[None, :] + deltas[:, 1:2]
    moved_z = coord_z[None, :] + deltas[:, 2:3]
    shift_x = jnp.floor_divide(moved_x, SIDE)
    shift_y = jnp.floor_divide(moved_y, SIDE)
    shift_z = jnp.floor_divide(moved_z, LZ)
    target_site = (moved_x - shift_x * SIDE) * (SIDE * LZ) + (moved_y - shift_y * SIDE) * LZ + (moved_z - shift_z * LZ)
    grid_x = jnp.arange(N_GX, dtype=jnp.int32)[:, None, None, None, None]
    grid_y = jnp.arange(N_GY, dtype=jnp.int32)[None, :, None, None, None]
    grid_z = jnp.arange(N_GZ, dtype=jnp.int32)[None, None, :, None, None]
    dest_x = (grid_x + shift_x[None, None, None]) % N_GX
    dest_y = (grid_y + shift_y[None, None, None]) % N_GY
    raw_z = grid_z + shift_z[None, None, None]
    inside = (raw_z >= 0) & (raw_z < N_GZ)
    dest_z = raw_z % N_GZ
    slot_pos = inverse[dest_x, dest_y, dest_z, target_site[None, None, None]]
    block = (shift_x + 1) * 9 + (shift_y + 1) * 3 + (shift_z + 1)
    is_local = (shift_x == 0) & (shift_y == 0) & (shift_z == 0)
    index = jnp.where(is_local[None, None, None], target_site[None, None, None], A + block[None, None, None] * G + slot_pos)
    key_rate, key_roll = jax.random.split(key)
    rates = jax.random.randint(key_rate, (N_GX, N_GY, N_GZ, 1, 1), 30, 101)
    rolls = jax.random.randint(key_roll, (N_GX, N_GY, N_GZ, K, A), 0, 100)
    keep = (rolls < rates) & inside
    return jnp.where(keep, index, -1).astype(jnp.int32)


def draw_positions(key, part):
    key = jax.random.fold_in(key, 5)
    lattice_ids, coord_x, coord_y, coord_z = lattice_coords()
    centres = jnp.stack([coord_x, coord_y, coord_z]).astype(jnp.float32) * SPACING + 0.5 * SPACING
    shape = (N_GX, N_GY, N_GZ, 3, A)
    jitter = jnp.clip(0.15 * jax.random.normal(key, shape, jnp.float32), -0.4, 0.4)
    return centres[None, None, None] + jitter


def touch_ends(values, rng, smallest, high):
    place = [jax.random.randint(jax.random.fold_in(rng, axis), (), 0, length) for axis, length in enumerate(values.shape)]
    widest = values.shape.index(max(values.shape))
    neighbour = place[:widest] + [(place[widest] + 1) % values.shape[widest]] + place[widest + 1:]
    return values.at[tuple(place)].set(smallest).at[tuple(neighbour)].set(high)


def noise(rng, extent, deviation, most, kind=jnp.bfloat16):
    values = deviation * jax.random.normal(rng, extent, jnp.float32)
    return jnp.clip(values, min=-most, max=most).astype(kind)


def setup_inputs(seed: int = 0) -> dict:
    key_of = jax.random.split(jax.random.key(seed), 14)
    positions = draw_positions(jax.random.fold_in(key_of[13], 71), 0)
    species = touch_ends(jax.random.randint(key_of[1], (N_GX, N_GY, N_GZ, A), 0, SPECIES), jax.random.fold_in(key_of[1], 1), 0, SPECIES - 1).astype(jnp.int32)
    send_rows = draw_send_rows(jax.random.fold_in(key_of[13], 71), 0)
    neighbours = draw_neighbours(jax.random.fold_in(key_of[13], 71), 0)
    embedding = noise(key_of[4], (SPECIES, C), 1.0, 6.0, jnp.float32)
    self_energy = noise(key_of[5], (SPECIES,), 1.0, 6.0, jnp.float32)
    source_weight = noise(key_of[6], (LAYERS, C, C), C ** -0.5, 0.5, jnp.float32)
    radial_in = noise(key_of[7], (LAYERS, NB, RH), 1 ** -0.5, 6.0, jnp.float32)
    radial_out = noise(key_of[8], (LAYERS, RH, 3 * C), RH ** -0.5, 0.75, jnp.float32)
    mix_weight = noise(key_of[9], (LAYERS, 3 * C, C), (3 * C) ** -0.5, 0.3125, jnp.float32)
    read_one = noise(key_of[10], (C,), C ** -0.5, 0.5, jnp.float32)
    read_hidden = noise(key_of[11], (C, RO), C ** -0.5, 0.5, jnp.float32)
    read_two = noise(key_of[12], (RO,), RO ** -0.5, 1.5, jnp.float32)
    return {"positions": positions, "species": species, "send_rows": send_rows, "neighbours": neighbours, "embedding": embedding, "self_energy": self_energy, "source_weight": source_weight, "radial_in": radial_in, "radial_out": radial_out, "mix_weight": mix_weight, "read_one": read_one, "read_hidden": read_hidden, "read_two": read_two}


PRECISE = lax.Precision.HIGHEST
CUTOFF = 6.0
SPACING = 2.5
SOFTEN = 0.25
MESSAGE_SCALE = 0.25
OFFSETS = np.array([[b // 9 - 1, b // 3 % 3 - 1, b % 3 - 1] for b in range(27)], np.int32)

def envelope(scaled):
    return 1.0 - 28.0 * scaled ** 6 + 48.0 * scaled ** 7 - 21.0 * scaled ** 8

def harmonics(direction):
    along_x = direction[0]
    along_y = direction[1]
    along_z = direction[2]
    root_three = math.sqrt(3.0)
    root_fifteen = math.sqrt(15.0)
    root_five = math.sqrt(5.0)
    degree_one = jnp.stack([root_three * along_x, root_three * along_y, root_three * along_z])
    degree_two = jnp.stack([root_fifteen * along_x * along_y, root_fifteen * along_y * along_z, 0.5 * root_five * (3.0 * along_z * along_z - 1.0), root_fifteen * along_x * along_z, 0.5 * root_fifteen * (along_x * along_x - along_y * along_y)])
    return (degree_one, degree_two)

def interaction(own_pos, table_pos, table_feat, neighbour_list, source_weight, radial_in, radial_out, mix_weight):
    own_count = own_pos.shape[1]
    slot_count = neighbour_list.shape[0]
    channels = table_feat.shape[1]
    usable = (neighbour_list >= 0).reshape(-1).astype(jnp.float32)
    column_ids = jnp.maximum(neighbour_list, 0).reshape(-1)
    centres = jnp.tile(own_pos, (1, slot_count))
    displace = table_pos[:, column_ids] - centres
    distance = jnp.sqrt(lax.optimization_barrier(jnp.sum(displace * displace, axis=0)) + SOFTEN)
    direction = displace / distance[None, :]
    scaled = jnp.minimum(distance / CUTOFF, 1.0)
    harmonic_orders = jnp.arange(1, radial_in.shape[0] + 1).astype(jnp.float32)
    radial_basis = math.sqrt(2.0 / CUTOFF) * jnp.sin(harmonic_orders[:, None] * (math.pi / CUTOFF) * distance[None, :]) / distance[None, :] * (envelope(scaled) * usable)[None, :]
    hidden = jax.nn.silu(jnp.dot(radial_basis.T, radial_in, precision=PRECISE))
    radial = jnp.dot(hidden, radial_out, precision=PRECISE)
    source = jnp.dot(table_feat, source_weight, precision=PRECISE)[column_ids]
    degree_one, degree_two = harmonics(direction)
    scalar_terms = (radial[:, :channels] * source).reshape(slot_count, own_count, channels)
    vector_terms = (radial[:, channels:2 * channels] * source).reshape(slot_count, own_count, channels)
    tensor_terms = (radial[:, 2 * channels:] * source).reshape(slot_count, own_count, channels)
    scalar = MESSAGE_SCALE * lax.optimization_barrier(jnp.sum(scalar_terms, axis=0))
    vector_part = MESSAGE_SCALE * jnp.einsum('mka,kac->mac', degree_one.reshape(3, slot_count, own_count), vector_terms, precision=PRECISE)
    tensor_part = MESSAGE_SCALE * jnp.einsum('mka,kac->mac', degree_two.reshape(5, slot_count, own_count), tensor_terms, precision=PRECISE)
    invariants = jnp.concatenate([scalar, lax.optimization_barrier(jnp.sum(vector_part * vector_part, axis=0)), lax.optimization_barrier(jnp.sum(tensor_part * tensor_part, axis=0))], axis=1)
    return table_feat[:own_count] + jnp.dot(invariants, mix_weight, precision=PRECISE)

def readout(feat_one, feat_two, read_one, read_hidden, read_two):
    inner = jax.nn.silu(jnp.dot(feat_two, read_hidden, precision=PRECISE))
    return jnp.dot(feat_one, read_one, precision=PRECISE) + jnp.dot(inner, read_two, precision=PRECISE)

def reference(positions, species, send_rows, neighbours, embedding, self_energy, source_weight, radial_in, radial_out, mix_weight, read_one, read_hidden, read_two):
    domains = N_GX * N_GY * N_GZ
    box_sides = jnp.array([SIDE * SPACING, SIDE * SPACING, LZ * SPACING], jnp.float32)
    shifts = jnp.array(OFFSETS, jnp.float32) * box_sides[None, :]
    offset_x = jnp.array(OFFSETS[:, 0], jnp.int32)
    offset_y = jnp.array(OFFSETS[:, 1], jnp.int32)
    offset_z = jnp.array(OFFSETS[:, 2], jnp.int32)
    flat_species = species.reshape(domains, A)
    flat_send = send_rows.reshape(domains, G)
    flat_lists = neighbours.reshape(domains, K, A)
    h_zero = embedding[flat_species]

    def domain_ids(index):
        index_x = index // (N_GY * N_GZ)
        index_y = index // N_GZ % N_GY
        index_z = index % N_GZ
        return ((index_x + offset_x) % N_GX * (N_GY * N_GZ) + (index_y + offset_y) % N_GY * N_GZ + (index_z + offset_z) % N_GZ).astype(jnp.int32)

    def energies(all_pos):
        flat_pos = all_pos.reshape(domains, 3, A)
        send_pos = jnp.take_along_axis(flat_pos, flat_send[:, None, :], axis=2)

        def layer_all(layer, feats):
            send_feat = jnp.take_along_axis(feats, flat_send[:, :, None], axis=1)

            def one_domain(index):
                ids = domain_ids(index)
                ghost_pos = (send_pos[ids] + shifts[:, :, None]).transpose(1, 0, 2).reshape(3, 27 * G)
                own_pos = flat_pos[index]
                table_pos = jnp.concatenate([own_pos, ghost_pos], axis=1)
                table_feat = jnp.concatenate([feats[index], send_feat[ids].reshape(27 * G, C)], axis=0)
                return interaction(own_pos, table_pos, table_feat, flat_lists[index], source_weight[layer], radial_in[layer], radial_out[layer], mix_weight[layer])
            return lax.map(jax.checkpoint(one_domain), jnp.arange(domains, dtype=jnp.int32))
        h_one = layer_all(0, h_zero)
        h_two = layer_all(1, h_one)
        totals = self_energy[flat_species] + readout(h_one, h_two, read_one, read_hidden, read_two)
        return totals.reshape(N_GX, N_GY, N_GZ, A)
    atom_energy, pullback = jax.vjp(energies, positions)
    gradient = pullback(jnp.ones_like(atom_energy))[0]
    return (atom_energy, -gradient)
```

```python
import functools
import math

import jax
import jax.numpy as jnp
from jax import lax
from jax.experimental import pallas as pl
from jax.experimental.pallas import tpu as pltpu
from jax.sharding import PartitionSpec as P

F32 = jnp.float32
BF16 = jnp.bfloat16
HIGHEST = lax.Precision.HIGHEST
MESH = pl.DeviceIdType.MESH
CUTOFF = 6.0
BOX = (7.5, 7.5, 5.0)
ATOMS = 18
SLOTS = 56
CHANNELS = 128
HIDDEN = 64
ORDERS = 8
ROWS = 24
TABLE = 28 * ROWS
EDGES = 1024
TILES = 8
CHUNK = 16
OWN = 13
OFFSETS = tuple((b // 9 - 1, b // 3 % 3 - 1, b % 3 - 1) for b in range(27))
OTHERS = tuple(b for b in range(27) if b != OWN)
NN = ((1,), (0,))
NT = ((1,), (1,))
TN = ((0,), (0,))


def dot(left, right, dims, precision=None):
    return lax.dot_general(
        left, right, (dims, ((), ())), precision=precision, preferred_element_type=F32
    )


def halves(value):
    high = value.astype(BF16).astype(F32)
    return high, value - high


def dot_split(left, right, dims):
    left_high, left_low = halves(left)
    right_high, right_low = halves(right)
    left_high = left_high.astype(BF16)
    right_high = right_high.astype(BF16)
    return (
        dot(left_high, right_high, dims)
        + dot(left_high, right_low.astype(BF16), dims)
        + dot(left_low.astype(BF16), right_high, dims)
    )


def iota(shape, dim):
    return lax.broadcasted_iota(jnp.int32, shape, dim)


def over(value, divisor):
    return (value * (65536 // divisor + 1)) >> 16


def lanes(index):
    return pl.ds(pl.multiple_of(index * 128, 128), 128)


def column(row, rows):
    return jnp.transpose(jnp.broadcast_to(row, (128, 128)))[0:rows]


def packed(values):
    row = values[0:1]
    for c in range(1, 4):
        row = row + pltpu.roll(values[c : c + 1], 32 * c, 1)
    return row


def unrolled(values, c):
    return values if c == 0 else pltpu.roll(values, 128 - 32 * c, 1)


def kernel(
    pos_ref,
    species_ref,
    send_ref,
    nbr_ref,
    emb_ref,
    self_ref,
    source_ref,
    rin_ref,
    rout_ref,
    mix_ref,
    read_one_ref,
    read_hidden_ref,
    read_two_ref,
    energy_ref,
    force_ref,
    stage,
    slots,
    table_emb,
    packet,
    arrived,
    leaving,
    returned,
    feat,
    feat_grad,
    feat_back,
    onehot,
    ghot,
    bhot,
    geo,
    basis_ref,
    dbasis_ref,
    harm,
    harm_grad,
    r_grad,
    radial,
    dsilu,
    source,
    source_grad,
    acc,
    expanded,
    grad_high,
    grad_low,
    sent,
    received,
):
    me = (lax.axis_index("gx"), lax.axis_index("gy"), lax.axis_index("gz"))
    extent = (3, 16, 16)

    def device(offset):
        return tuple(lax.rem(m + (o + n), n) for m, o, n in zip(me, offset, extent))

    def minus(offset):
        return tuple(-o for o in offset)

    barrier = pltpu.get_barrier_semaphore()
    for b in OTHERS:
        pl.semaphore_signal(barrier, inc=1, device_id=device(OFFSETS[b]), device_id_type=MESH)

    def remote(phase, index, src, dst, offset):
        return pltpu.make_async_remote_copy(
            src_ref=src,
            dst_ref=dst,
            send_sem=sent.at[phase, index],
            recv_sem=received.at[phase, index],
            device_id=device(offset),
            device_id_type=MESH,
        )

    stage[...] = jnp.zeros_like(stage)
    stage[0:3, 0:ATOMS] = pos_ref[0, 0, 0]
    stage[3:4, 0:ATOMS] = species_ref[0, 0].astype(F32)
    stage[8:9, 0:ATOMS] = send_ref[0, 0].astype(F32)
    lane = iota((128, 128), 1)
    row = iota((128, 128), 0)
    send_row = jnp.where(lane[0:1] < ATOMS, stage[8:9], -5.0)
    own = stage[0:8]
    to_send = (row.astype(F32) == send_row).astype(F32)
    own_send = dot(own, to_send, NN, HIGHEST)
    packet[0] = packed(own_send)
    arrived[OWN] = packed(own)
    arrived[27:32] = jnp.zeros((5, 1, 128), F32)
    pl.semaphore_wait(barrier, 26)
    first = [
        remote(0, b, packet.at[0], arrived.at[b], minus(OFFSETS[b])) for b in OTHERS
    ]
    for copy in first:
        copy.start()

    send_col = column(send_row, 128)
    lane_atom = jnp.where(lane < 7 * ATOMS, lane - ATOMS * over(lane, ATOMS), -7)
    select = (send_col[0:ROWS] == lane_atom[0:ROWS].astype(F32)).astype(F32)
    select_wide = jnp.concatenate([select, select], axis=1).astype(BF16)
    select_deep = jnp.concatenate([select, select], axis=0).astype(BF16)
    unsend = (send_col == lane.astype(F32)).astype(F32)
    spread = (row == lane_atom).astype(F32)
    centre = dot(own, spread, NN, HIGHEST)

    slots[...] = jnp.zeros_like(slots)
    slots[:, 0:ATOMS] = (nbr_ref[0, 0, 0] + 1).astype(F32)
    named = slots[0:8]
    for j in range(1, 7):
        named = named + pltpu.roll(slots[8 * j : 8 * j + 8], ATOMS * j, 1)
    named = named.astype(jnp.int32) - 1
    outer = jnp.maximum(named - ATOMS, 0)
    block = jnp.where(named < 0, -1, jnp.where(named < ATOMS, OWN, over(outer, ATOMS)))
    member = jnp.where(named < ATOMS, named, outer - ATOMS * over(outer, ATOMS))
    usable = (named >= 0).astype(F32)

    table_row = iota((TABLE, 128), 0)
    table_block = over(table_row, ROWS)
    table_member = table_row - ROWS * table_block
    label = jnp.where(
        (table_member < ATOMS) & (table_block < 27),
        ATOMS + ATOMS * table_block + table_member,
        -2,
    )
    label = jnp.concatenate(
        [label[0 : OWN * ROWS], send_col[0:ROWS].astype(jnp.int32), label[(OWN + 1) * ROWS :]],
        axis=0,
    )
    for k in range(TILES):
        tile = slice(128 * k, 128 * k + 128)
        onehot[:, tile] = (label == named[k : k + 1]).astype(F32).astype(BF16)
        ghot[:, tile] = (row == member[k : k + 1]).astype(F32).astype(BF16)
        bhot[k] = (row[0:32] == block[k : k + 1]).astype(F32)

    table_emb[...] = jnp.zeros_like(table_emb)
    table_emb[0:89] = emb_ref[...]
    table_emb[128:129, 0:89] = self_ref[...]
    embedding = table_emb[0:128]
    species_col = column(own_send[3:4], ROWS)
    own_hot = (
        (species_col == lane[0:ROWS].astype(F32)) & (row[0:ROWS] < ATOMS)
    ).astype(F32)
    h_zero = dot(own_hot, embedding, NN, HIGHEST)
    isolated = jnp.sum(own_hot * table_emb[128:129], axis=1, keepdims=True)
    emb_source = dot_split(jnp.transpose(source_ref[0]), embedding, NT)
    emb_source = jnp.concatenate(halves(emb_source), axis=0).astype(BF16)

    rin_high, rin_low = halves(jnp.concatenate([rin_ref[0], rin_ref[1]], axis=1))
    rin_wide = jnp.concatenate(
        [rin_high, rin_high, rin_low, jnp.zeros((104, 128), F32)], axis=0
    )
    rin_wide = jnp.transpose(rin_wide)[:, 0:32].astype(BF16)
    rin_back = []
    rout_wide = []
    rout_back = []
    for t in range(2):
        high, low = halves(rout_ref[t])
        rout_wide.append(
            jnp.transpose(jnp.concatenate([high, high, low, low], axis=0)).astype(BF16)
        )
        rout_back.append(jnp.concatenate([high, low], axis=0).astype(BF16))
        high, low = halves(rin_ref[t])
        rin_back.append(jnp.concatenate([high, low], axis=0).astype(BF16))

    for copy in first:
        copy.wait_recv()
    lane_part = over(lane[0:32], 32)
    domain = row[0:32]
    third = over(domain, 3)
    shift = jnp.where(
        lane_part == 0,
        (over(domain, 9) - 1).astype(F32) * BOX[0],
        jnp.where(
            lane_part == 1,
            (third - 3 * over(domain, 9) - 1).astype(F32) * BOX[1],
            jnp.where(lane_part == 2, (domain - 3 * third - 1).astype(F32) * BOX[2], 0.0),
        ),
    )
    nearby = arrived[...].reshape(32, 128) + shift
    nearby = jnp.concatenate([unrolled(nearby, c) for c in range(4)], axis=0)
    high, low = halves(nearby)
    middle, low = halves(low)
    nearby = jnp.concatenate([high, middle, low], axis=0).astype(BF16)
    by_block = dot(nearby, ghot[...], NN)
    by_block = by_block[0:128] + by_block[128:256] + by_block[256:384]
    for k in range(TILES):
        tile = slice(128 * k, 128 * k + 128)
        for c in range(4):
            geo[c, k : k + 1, :] = jnp.sum(
                by_block[32 * c : 32 * c + 32, tile] * bhot[k], axis=0, keepdims=True
            )

    dx = geo[0] - centre[0:1]
    dy = geo[1] - centre[1:2]
    dz = geo[2] - centre[2:3]
    distance = jnp.sqrt(dx * dx + dy * dy + dz * dz + 0.25)
    inverse = 1.0 / distance
    nx = dx * inverse
    ny = dy * inverse
    nz = dz * inverse
    scaled = jnp.minimum(distance * (1.0 / CUTOFF), 1.0)
    square = scaled * scaled
    fifth = square * square * scaled
    sixth = fifth * scaled
    seventh = sixth * scaled
    envelope = 1.0 - 28.0 * sixth + 48.0 * seventh - 21.0 * seventh * scaled
    envelope_grad = (-168.0 * fifth + 336.0 * sixth - 168.0 * seventh) * (1.0 / CUTOFF)
    weight = math.sqrt(2.0 / CUTOFF) * inverse * usable
    weight_grad = weight * (envelope_grad - envelope * inverse)
    weight = weight * envelope
    angle = distance * (math.pi / CUTOFF)
    sine_one = jnp.sin(angle)
    cosine_one = jnp.cos(angle)
    sine, cosine = sine_one, cosine_one
    sine_last, cosine_last = jnp.zeros_like(angle), jnp.ones_like(angle)
    for m in range(ORDERS):
        basis_ref[:, m, :] = weight * sine
        dbasis_ref[:, m, :] = weight_grad * sine + weight * cosine * ((m + 1) * math.pi / CUTOFF)
        sine, sine_last = 2.0 * cosine_one * sine - sine_last, sine
        cosine, cosine_last = 2.0 * cosine_one * cosine - cosine_last, cosine
    r3, r5, r15 = math.sqrt(3.0), math.sqrt(5.0), math.sqrt(15.0)
    for m, value in enumerate(
        (
            r3 * nx,
            r3 * ny,
            r3 * nz,
            r15 * nx * ny,
            r15 * ny * nz,
            0.5 * r5 * (3.0 * nz * nz - 1.0),
            r15 * nx * nz,
            0.5 * r15 * (nx * nx - ny * ny),
        )
    ):
        harm[:, m, :] = value

    basis = jnp.concatenate([basis_ref[k] for k in range(TILES)], axis=1)
    high, low = halves(basis)
    basis = jnp.concatenate([high, low, high, jnp.zeros_like(high)], axis=0).astype(BF16)
    pre = dot(rin_wide, basis, NN)
    gate = 1.0 / (1.0 + jnp.exp(-pre))
    hidden = pre * gate
    dsilu[...] = gate * (1.0 + pre * (1.0 - gate))
    hidden_high, hidden_low = halves(hidden)

    def radial_layer(t):
        rows = slice(HIDDEN * t, HIDDEN * t + HIDDEN)
        deep = jnp.concatenate(
            [hidden_high[rows], hidden_low[rows], hidden_high[rows], hidden_low[rows]], axis=0
        )
        radial[t] = dot(rout_wide[t], deep.astype(BF16), NN)

    def gather_sum(t):
        def chunk(ci, carry):
            c0 = pl.multiple_of(ci * CHUNK, CHUNK)
            rows = [pl.ds(pl.multiple_of(128 * q + c0, CHUNK), CHUNK) for q in range(3)]
            sums = [None] * 9
            for k in range(TILES):
                tile = slice(128 * k, 128 * k + 128)
                src = source[t, rows[0], tile]
                terms = [radial[t, rows[q], tile] * src for q in range(3)]
                ys = harm[k]
                parts = [terms[0]]
                parts += [terms[1] * ys[m : m + 1] for m in range(3)]
                parts += [terms[2] * ys[m : m + 1] for m in range(3, 8)]
                sums = [p if s is None else s + p for s, p in zip(sums, parts)]
            for i in range(9):
                acc[i, rows[0], :] = sums[i]
            return carry

        lax.fori_loop(0, CHANNELS // CHUNK, chunk, 0)

    def interaction(t, feats):
        gather_sum(t)
        wide = acc[...].reshape(9 * 128, 128)
        wide = jnp.concatenate(halves(wide), axis=1).astype(BF16)
        moments = 0.25 * dot(select_wide, wide, NT)
        parts = [moments[:, 128 * i : 128 * i + 128] for i in range(9)]
        vector = parts[1] * parts[1] + parts[2] * parts[2] + parts[3] * parts[3]
        tensor = parts[4] * parts[4]
        for i in range(5, 9):
            tensor = tensor + parts[i] * parts[i]
        invariants = jnp.concatenate([parts[0], vector, tensor], axis=1)
        return feats + dot_split(invariants, mix_ref[t], NN), parts

    def interaction_back(t, grad, parts, with_source):
        inv_grad = dot_split(grad, mix_ref[t], NT)
        grads = [0.25 * inv_grad[:, 0:128]]
        grads += [0.5 * inv_grad[:, 128:256] * parts[i] for i in range(1, 4)]
        grads += [0.5 * inv_grad[:, 256:384] * parts[i] for i in range(4, 9)]
        deep = jnp.concatenate(grads, axis=1)
        deep = jnp.concatenate(halves(deep), axis=0).astype(BF16)
        expanded[...] = dot(deep, select_deep, TN).reshape(9, 128, 128)

        def tile_back(k, carry):
            tile = lanes(k)
            ys = harm[k]
            sums = [jnp.zeros((8, 128), F32)] * 8
            for ci in range(CHANNELS // CHUNK):
                rows = [slice(128 * q + CHUNK * ci, 128 * q + CHUNK * ci + CHUNK) for q in range(3)]
                src = source[t, rows[0], tile]
                rads = [radial[t, rows[q], tile] for q in range(3)]
                wide = [expanded[i, rows[0], :] for i in range(9)]
                pulls = [wide[0], wide[1] * ys[0:1], wide[4] * ys[3:4]]
                for m in range(1, 3):
                    pulls[1] = pulls[1] + wide[1 + m] * ys[m : m + 1]
                for m in range(4, 8):
                    pulls[2] = pulls[2] + wide[1 + m] * ys[m : m + 1]
                if with_source:
                    high, low = halves(
                        rads[0] * pulls[0] + rads[1] * pulls[1] + rads[2] * pulls[2]
                    )
                    source_grad[rows[0], tile] = high.astype(BF16)
                    source_grad[rows[1], tile] = low.astype(BF16)
                for q in range(3):
                    high, low = halves(src * pulls[q])
                    grad_high[rows[q], tile] = high.astype(BF16)
                    grad_low[rows[q], tile] = low.astype(BF16)
                for m in range(8):
                    value = wide[1 + m] * (rads[1 if m < 3 else 2] * src)
                    sums[m] = sums[m] + (value[0:8] + value[8:16])
            tops = [jnp.sum(s, axis=0, keepdims=True) for s in sums]
            harm_grad[t, k] = jnp.concatenate(tops, axis=0)
            return carry

        lax.fori_loop(0, TILES, tile_back, 0)

    def radial_back(t):
        rows = slice(HIDDEN * t, HIDDEN * t + HIDDEN)
        both = dot(rout_back[t], grad_high[...], NN)
        grad = both[0:HIDDEN] + both[HIDDEN : 2 * HIDDEN]
        grad = grad + dot(rout_back[t][0:HIDDEN], grad_low[...], NN)
        high, low = halves(grad * dsilu[rows])
        both = dot(rin_back[t], high.astype(BF16), NN)
        grad = both[0:ORDERS] + both[ORDERS : 2 * ORDERS]
        grad = grad + dot(rin_back[t][0:ORDERS], low.astype(BF16), NN)
        for k in range(TILES):
            r_grad[t, k : k + 1, :] = jnp.sum(
                grad[:, 128 * k : 128 * k + 128] * dbasis_ref[k], axis=0, keepdims=True
            )

    radial_layer(0)
    element = geo[3]
    for k in range(TILES):
        tile = slice(128 * k, 128 * k + 128)
        hot = (row.astype(F32) == element[k : k + 1]).astype(F32).astype(BF16)
        both = dot(emb_source, hot, NN)
        source[0, :, tile] = both[0:128] + both[128:256]
    h_one, parts_one = interaction(0, h_zero)

    feat[OWN] = dot_split(h_one, source_ref[1], NN)
    feat[27] = jnp.zeros((ROWS, 128), F32)
    second = [
        remote(1, b, feat.at[OWN], feat.at[b], minus(OFFSETS[b])) for b in OTHERS
    ]
    for copy in second:
        copy.start()
    radial_layer(1)
    for copy in second:
        copy.wait_recv()

    table = jnp.transpose(feat[...].reshape(TABLE, 128))
    table = jnp.concatenate(halves(table), axis=0).astype(BF16)
    both = dot(table, onehot[...], NN)
    source[1] = both[0:128] + both[128:256]
    h_two, parts_two = interaction(1, h_one)
    inner = dot_split(h_two, read_hidden_ref[...], NN)
    gate = 1.0 / (1.0 + jnp.exp(-inner))
    learned = jnp.sum(h_one * read_one_ref[...], axis=1, keepdims=True) + jnp.sum(
        inner * gate * read_two_ref[...], axis=1, keepdims=True
    )
    energy = jnp.sum((isolated + learned) * unsend[0:ROWS], axis=0, keepdims=True)
    energy_ref[0, 0] = energy[:, 0:ATOMS]
    inner_grad = gate * (1.0 + inner * (1.0 - gate)) * read_two_ref[...]
    grad_two = dot_split(inner_grad, read_hidden_ref[...], NT)
    interaction_back(1, grad_two, parts_two, True)

    both = dot(onehot[...], source_grad[...], NT)
    feat_grad[...] = (both[:, 0:128] + both[:, 128:256]).reshape(28, ROWS, 128)
    third_copies = [
        remote(2, b, feat_grad.at[b], feat_back.at[b], OFFSETS[b]) for b in OTHERS
    ]
    for copy in third_copies:
        copy.start()
    radial_back(1)
    for copy in third_copies:
        copy.wait_recv()
    total = feat_grad[OWN]
    for b in OTHERS:
        total = total + feat_back[b]
    grad_one = grad_two + read_one_ref[...] + dot_split(total, source_ref[1], NT)

    interaction_back(0, grad_one, parts_one, False)
    radial_back(0)

    pulls = [harm_grad[0, :, m, :] + harm_grad[1, :, m, :] for m in range(8)]
    along = r_grad[0] + r_grad[1]
    gx = r3 * pulls[0] + r15 * (ny * pulls[3] + nz * pulls[6] + nx * pulls[7])
    gy = r3 * pulls[1] + r15 * (nx * pulls[3] + nz * pulls[4] - ny * pulls[7])
    gz = r3 * pulls[2] + r15 * (ny * pulls[4] + nx * pulls[6]) + 3.0 * r5 * nz * pulls[5]
    radially = along - (nx * gx + ny * gy + nz * gz) * inverse
    pulls = [radially * n + g * inverse for n, g in ((nx, gx), (ny, gy), (nz, gz))]
    highs = []
    for k in range(TILES):
        blocks = jnp.concatenate([bhot[k] * p[k : k + 1] for p in pulls], axis=0)
        highs.append(jnp.concatenate(halves(blocks), axis=0))
    blocks = jnp.concatenate(highs, axis=1).astype(BF16)
    both = dot(blocks, ghot[...], NT)
    both = both[0:96] + both[96:192]
    rows = both[0:32]
    for c in range(1, 3):
        rows = rows + pltpu.roll(both[32 * c : 32 * c + 32], 32 * c, 1)
    for b in range(27):
        leaving[b] = rows[b : b + 1]
    fourth = [
        remote(3, b, leaving.at[b], returned.at[b], OFFSETS[b]) for b in OTHERS
    ]
    for copy in fourth:
        copy.start()
    sums = [jnp.sum(p, axis=0, keepdims=True) for p in pulls] + [jnp.zeros((5, 128), F32)]
    force = dot(jnp.concatenate(sums, axis=0), spread, NT, HIGHEST)
    own_row = rows[OWN : OWN + 1]
    force = force - jnp.concatenate([unrolled(own_row, c) for c in range(3)] + [sums[3]], axis=0)
    for copy in fourth:
        copy.wait_recv()
    back = returned[OTHERS[0]]
    for b in OTHERS[1:]:
        back = back + returned[b]
    back = jnp.concatenate([unrolled(back, c) for c in range(3)] + [sums[3]], axis=0)
    force = force - dot(back, unsend, NN, HIGHEST)
    force_ref[0, 0, 0] = force[0:3, 0:ATOMS]
    for copy in first + second + third_copies + fourth:
        copy.wait_send()


def per_device(
    positions,
    species,
    send_rows,
    neighbours,
    embedding,
    self_energy,
    source_weight,
    radial_in,
    radial_out,
    mix_weight,
    read_one,
    read_hidden,
    read_two,
):
    vmem = pl.BlockSpec(memory_space=pltpu.VMEM)
    energy, forces = pl.pallas_call(
        kernel,
        out_shape=(
            jax.ShapeDtypeStruct((1, 1, 1, ATOMS), F32),
            jax.ShapeDtypeStruct((1, 1, 1, 3, ATOMS), F32),
        ),
        in_specs=[vmem] * 13,
        out_specs=(vmem, vmem),
        scratch_shapes=[
            pltpu.VMEM((16, 128), F32),
            pltpu.VMEM((SLOTS, 128), F32),
            pltpu.VMEM((136, 128), F32),
            pltpu.VMEM((1, 1, 128), F32),
            pltpu.VMEM((32, 1, 128), F32),
            pltpu.VMEM((27, 1, 128), F32),
            pltpu.VMEM((27, 1, 128), F32),
            pltpu.VMEM((28, ROWS, 128), F32),
            pltpu.VMEM((28, ROWS, 128), F32),
            pltpu.VMEM((27, ROWS, 128), F32),
            pltpu.VMEM((TABLE, EDGES), BF16),
            pltpu.VMEM((128, EDGES), BF16),
            pltpu.VMEM((TILES, 32, 128), F32),
            pltpu.VMEM((4, 8, 128), F32),
            pltpu.VMEM((TILES, ORDERS, 128), F32),
            pltpu.VMEM((TILES, ORDERS, 128), F32),
            pltpu.VMEM((TILES, 8, 128), F32),
            pltpu.VMEM((2, TILES, 8, 128), F32),
            pltpu.VMEM((2, TILES, 128), F32),
            pltpu.VMEM((2, 384, EDGES), F32),
            pltpu.VMEM((128, EDGES), F32),
            pltpu.VMEM((2, 128, EDGES), F32),
            pltpu.VMEM((256, EDGES), BF16),
            pltpu.VMEM((9, 128, 128), F32),
            pltpu.VMEM((9, 128, 128), F32),
            pltpu.VMEM((384, EDGES), BF16),
            pltpu.VMEM((384, EDGES), BF16),
            pltpu.SemaphoreType.DMA((4, 27)),
            pltpu.SemaphoreType.DMA((4, 27)),
        ],
        compiler_params=pltpu.CompilerParams(
            collective_id=0, has_side_effects=True, vmem_limit_bytes=48 * 1024 * 1024
        ),
        name="energy_and_forces",
    )(
        positions,
        species,
        send_rows,
        neighbours,
        embedding,
        self_energy[None],
        source_weight,
        radial_in,
        radial_out,
        mix_weight,
        read_one[None],
        read_hidden,
        read_two[None],
    )
    return energy, forces


def solution(mesh):
    return jax.shard_map(
        per_device,
        mesh=mesh,
        in_specs=(
            P("gx", "gy", "gz", None, None),
            P("gx", "gy", "gz", None),
            P("gx", "gy", "gz", None),
            P("gx", "gy", "gz", None, None),
            P(),
            P(),
            P(),
            P(),
            P(),
            P(),
            P(),
            P(),
            P(),
        ),
        out_specs=(P("gx", "gy", "gz", None), P("gx", "gy", "gz", None, None)),
        check_vma=False,
    )
```

```python
import functools
import math

import jax
import jax.numpy as jnp
from jax import lax
from jax.experimental import pallas as pl
from jax.experimental.pallas import tpu as pltpu
from jax.sharding import PartitionSpec as P

F32 = jnp.float32
BF16 = jnp.bfloat16
HIGHEST = lax.Precision.HIGHEST
MESH = pl.DeviceIdType.MESH
CUTOFF = 6.0
BOX = (7.5, 7.5, 5.0)
ATOMS = 18
SLOTS = 56
CHANNELS = 128
HIDDEN = 64
ORDERS = 8
ROWS = 24
TABLE = 28 * ROWS
EDGES = 1024
TILES = 8
CHUNK = 16
OWN = 13
OFFSETS = tuple((b // 9 - 1, b // 3 % 3 - 1, b % 3 - 1) for b in range(27))
OTHERS = tuple(
    sorted(
        (b for b in range(27) if b != OWN),
        key=lambda b: -sum(abs(o) * w for o, w in zip(OFFSETS[b], (2, 1, 4))),
    )
)
NN = ((1,), (0,))
NT = ((1,), (1,))
TN = ((0,), (0,))


def dot(left, right, dims, precision=None):
    return lax.dot_general(
        left, right, (dims, ((), ())), precision=precision, preferred_element_type=F32
    )


def pick(value, selector, dims):
    high, low = halves(value)
    middle, low = halves(low)
    parts = jnp.concatenate([high, middle, low, jnp.zeros_like(low)], axis=0).astype(BF16)
    parts = dot(parts, selector.astype(BF16), dims)
    return (parts[0:8] + parts[8:16]) + parts[16:24]


def halves(value):
    high = value.astype(BF16).astype(F32)
    return high, value - high


def dot_split(left, right, dims):
    left_high, left_low = halves(left)
    right_high, right_low = halves(right)
    left_high = left_high.astype(BF16)
    right_high = right_high.astype(BF16)
    return (
        dot(left_high, right_high, dims)
        + dot(left_high, right_low.astype(BF16), dims)
        + dot(left_low.astype(BF16), right_high, dims)
    )


def iota(shape, dim):
    return lax.broadcasted_iota(jnp.int32, shape, dim)


def over(value, divisor):
    return (value * (65536 // divisor + 1)) >> 16


def lanes(index):
    return pl.ds(pl.multiple_of(index * 128, 128), 128)


def column(row, rows):
    return jnp.transpose(jnp.broadcast_to(row, (128, 128)))[0:rows]


def packed(values):
    row = values[0:1]
    for c in range(1, 4):
        row = row + pltpu.roll(values[c : c + 1], 32 * c, 1)
    return row


def unrolled(values, c):
    return values if c == 0 else pltpu.roll(values, 128 - 32 * c, 1)


def kernel(
    pos_ref,
    species_ref,
    send_ref,
    nbr_ref,
    emb_hbm,
    self_ref,
    source_hbm,
    rin_hbm,
    rout_hbm,
    mix_hbm,
    read_one_ref,
    read_hidden_ref,
    read_two_ref,
    energy_ref,
    force_ref,
    emb_ref,
    source_ref,
    rin_ref,
    rout_ref,
    mix_ref,
    stage,
    slots,
    table_emb,
    packet,
    arrived,
    leaving,
    returned,
    mine,
    feat,
    table,
    feat_grad,
    feat_back,
    onehot,
    ghot,
    bhot,
    geo,
    basis_ref,
    dbasis_ref,
    harm,
    edge_grad,
    radial,
    slope,
    term,
    dsilu,
    later,
    source,
    source_grad,
    acc,
    expanded,
    sent,
    received,
    loaded,
):
    me = (lax.axis_index("gx"), lax.axis_index("gy"), lax.axis_index("gz"))
    extent = (3, 16, 16)

    def device(offset):
        return tuple(lax.rem(m + (o + n), n) for m, o, n in zip(me, offset, extent))

    def minus(offset):
        return tuple(-o for o in offset)

    inputs = [
        pltpu.make_async_copy(src, dst, loaded.at[i])
        for i, (src, dst) in enumerate(
            (
                (emb_hbm, emb_ref),
                (source_hbm, source_ref),
                (rin_hbm, rin_ref),
                (rout_hbm, rout_ref),
                (mix_hbm, mix_ref),
            )
        )
    ]
    barrier = pltpu.get_barrier_semaphore()
    for b in OTHERS:
        pl.semaphore_signal(barrier, inc=1, device_id=device(OFFSETS[b]), device_id_type=MESH)
    for copy in inputs:
        copy.start()

    def remote(phase, index, src, dst, offset):
        return pltpu.make_async_remote_copy(
            src_ref=src,
            dst_ref=dst,
            send_sem=sent.at[phase, index],
            recv_sem=received.at[phase, index],
            device_id=device(offset),
            device_id_type=MESH,
        )

    stage[...] = jnp.zeros_like(stage)
    for c in range(3):
        stage[c : c + 1, 0:ATOMS] = pos_ref[0, 0, c]
    stage[3:4, 0:ATOMS] = species_ref[0, 0].astype(F32)
    stage[8:9, 0:ATOMS] = send_ref[0, 0].astype(F32)
    lane = iota((128, 128), 1)
    row = iota((128, 128), 0)
    send_row = jnp.where(lane[0:1] < ATOMS, stage[8:9], -5.0)
    own = stage[0:8]
    to_send = (row.astype(F32) == send_row).astype(F32)
    own_send = pick(own, to_send, NN)
    packet[0] = packed(own_send)
    arrived[OWN] = packed(own)
    arrived[27:32] = jnp.zeros((5, 1, 128), F32)
    pl.semaphore_wait(barrier, 26)
    first = [
        remote(0, b, packet.at[0], arrived.at[b], minus(OFFSETS[b])) for b in OTHERS
    ]
    for copy in first:
        copy.start()

    send_col = column(send_row, 128)
    lane_atom = jnp.where(lane < 7 * ATOMS, lane - ATOMS * over(lane, ATOMS), -7)
    select = (send_col[0:ROWS] == lane_atom[0:ROWS].astype(F32)).astype(F32)
    select_wide = jnp.concatenate([select, select], axis=1).astype(BF16)
    select_deep = jnp.concatenate([select, select], axis=0).astype(BF16)
    unsend = (send_col == lane.astype(F32)).astype(F32)
    spread = (row == lane_atom).astype(F32)
    centre = pick(own, spread, NN)

    slots[...] = jnp.zeros_like(slots)
    for a in range(ATOMS):
        slots[a : a + 1, 0:SLOTS] = (nbr_ref[0, 0, a] + 1).astype(F32)
    by_slot = jnp.transpose(slots[...])
    named = by_slot[0:8]
    for j in range(1, 7):
        named = named + pltpu.roll(by_slot[8 * j : 8 * j + 8], ATOMS * j, 1)
    named = named.astype(jnp.int32) - 1
    outer = jnp.maximum(named - ATOMS, 0)
    block = jnp.where(named < 0, -1, jnp.where(named < ATOMS, OWN, over(outer, ATOMS)))
    member = jnp.where(named < ATOMS, named, outer - ATOMS * over(outer, ATOMS))
    usable = (named >= 0).astype(F32)

    table_row = iota((TABLE, 128), 0)
    table_block = over(table_row, ROWS)
    table_member = table_row - ROWS * table_block
    label = jnp.where(
        (table_member < ATOMS) & (table_block < 27),
        ATOMS + ATOMS * table_block + table_member,
        -2,
    )
    label = jnp.concatenate(
        [label[0 : OWN * ROWS], send_col[0:ROWS].astype(jnp.int32), label[(OWN + 1) * ROWS :]],
        axis=0,
    )
    for k in range(TILES):
        tile = slice(128 * k, 128 * k + 128)
        onehot[:, tile] = (label == named[k : k + 1]).astype(F32).astype(BF16)
        ghot[:, tile] = (row == member[k : k + 1]).astype(F32).astype(BF16)
        bhot[k] = (row[0:32] == block[k : k + 1]).astype(F32)

    table_emb[...] = jnp.zeros_like(table_emb)
    for copy in inputs:
        copy.wait()
    table_emb[0:89] = emb_ref[...]
    table_emb[128:129, 0:89] = self_ref[...]
    embedding = table_emb[0:128]
    species_col = column(own_send[3:4], ROWS)
    own_hot = (
        (species_col == lane[0:ROWS].astype(F32)) & (row[0:ROWS] < ATOMS)
    ).astype(F32)
    h_zero = dot(own_hot, embedding, NN, HIGHEST)
    isolated = jnp.sum(own_hot * table_emb[128:129], axis=1, keepdims=True)
    emb_source = dot_split(jnp.transpose(source_ref[0]), embedding, NT)
    emb_source = jnp.concatenate(halves(emb_source), axis=0).astype(BF16)

    rin_high, rin_low = halves(jnp.concatenate([rin_ref[0], rin_ref[1]], axis=1))
    rin_wide = jnp.concatenate(
        [rin_high, rin_high, rin_low, jnp.zeros((104, 128), F32)], axis=0
    )
    rin_wide = jnp.transpose(rin_wide)[:, 0:32].astype(BF16)
    rout_wide = []
    for t in range(2):
        high, low = halves(rout_ref[t])
        rout_wide.append(
            jnp.transpose(jnp.concatenate([high, high, low, low], axis=0)).astype(BF16)
        )

    for copy in first:
        copy.wait_recv()
    lane_part = over(lane[0:32], 32)
    domain = row[0:32]
    third = over(domain, 3)
    shift = jnp.where(
        lane_part == 0,
        (over(domain, 9) - 1).astype(F32) * BOX[0],
        jnp.where(
            lane_part == 1,
            (third - 3 * over(domain, 9) - 1).astype(F32) * BOX[1],
            jnp.where(lane_part == 2, (domain - 3 * third - 1).astype(F32) * BOX[2], 0.0),
        ),
    )
    nearby = arrived[...].reshape(32, 128) + shift
    nearby = jnp.concatenate([unrolled(nearby, c) for c in range(4)], axis=0)
    high, low = halves(nearby)
    middle, low = halves(low)
    nearby = jnp.concatenate([high, middle, low], axis=0).astype(BF16)
    by_block = dot(nearby, ghot[...], NN)
    by_block = by_block[0:128] + by_block[128:256] + by_block[256:384]
    for k in range(TILES):
        tile = slice(128 * k, 128 * k + 128)
        for c in range(4):
            geo[c, k : k + 1, :] = jnp.sum(
                by_block[32 * c : 32 * c + 32, tile] * bhot[k], axis=0, keepdims=True
            )

    dx = geo[0] - centre[0:1]
    dy = geo[1] - centre[1:2]
    dz = geo[2] - centre[2:3]
    distance = jnp.sqrt(dx * dx + dy * dy + dz * dz + 0.25)
    inverse = 1.0 / distance
    nx = dx * inverse
    ny = dy * inverse
    nz = dz * inverse
    scaled = jnp.minimum(distance * (1.0 / CUTOFF), 1.0)
    square = scaled * scaled
    fifth = square * square * scaled
    sixth = fifth * scaled
    seventh = sixth * scaled
    envelope = 1.0 - 28.0 * sixth + 48.0 * seventh - 21.0 * seventh * scaled
    envelope_grad = (-168.0 * fifth + 336.0 * sixth - 168.0 * seventh) * (1.0 / CUTOFF)
    weight = math.sqrt(2.0 / CUTOFF) * inverse * usable
    weight_grad = weight * (envelope_grad - envelope * inverse)
    weight = weight * envelope
    angle = distance * (math.pi / CUTOFF)
    sine_one = jnp.sin(angle)
    cosine_one = jnp.cos(angle)
    sine, cosine = sine_one, cosine_one
    sine_last, cosine_last = jnp.zeros_like(angle), jnp.ones_like(angle)
    for m in range(ORDERS):
        basis_ref[:, m, :] = weight * sine
        dbasis_ref[:, m, :] = weight_grad * sine + weight * cosine * ((m + 1) * math.pi / CUTOFF)
        sine, sine_last = 2.0 * cosine_one * sine - sine_last, sine
        cosine, cosine_last = 2.0 * cosine_one * cosine - cosine_last, cosine
    r3, r5, r15 = math.sqrt(3.0), math.sqrt(5.0), math.sqrt(15.0)
    for m, value in enumerate(
        (
            r3 * nx,
            r3 * ny,
            r3 * nz,
            r15 * nx * ny,
            r15 * ny * nz,
            0.5 * r5 * (3.0 * nz * nz - 1.0),
            r15 * nx * nz,
            0.5 * r15 * (nx * nx - ny * ny),
        )
    ):
        harm[:, m, :] = value

    basis = jnp.concatenate([basis_ref[k] for k in range(TILES)], axis=1)


    def radial_in(value):
        high, low = halves(value)
        value = jnp.concatenate([high, low, high, jnp.zeros_like(high)], axis=0).astype(BF16)
        return dot(rin_wide, value, NN)

    pre = radial_in(basis)
    gate = 1.0 / (1.0 + jnp.exp(-pre))
    hidden = pre * gate
    dsilu[...] = gate * (1.0 + pre * (1.0 - gate))
    later[...] = hidden[HIDDEN : 2 * HIDDEN]

    def radial_out(t, value):
        high, low = halves(value[HIDDEN * t : HIDDEN * t + HIDDEN])
        deep = jnp.concatenate([high, low, high, low], axis=0).astype(BF16)
        return dot(rout_wide[t], deep, NN)

    def gather_sum(t):
        def chunk(ci, carry):
            c0 = pl.multiple_of(ci * CHUNK, CHUNK)
            rows = [pl.ds(pl.multiple_of(128 * q + c0, CHUNK), CHUNK) for q in range(3)]
            sums = [None] * 9
            for k in range(TILES):
                tile = slice(128 * k, 128 * k + 128)
                src = source[t, rows[0], tile]
                terms = [radial[t, rows[q], tile] * src for q in range(3)]
                term[t, rows[0], tile] = terms[1]
                term[t, rows[1], tile] = terms[2]
                ys = harm[k]
                parts = [terms[0]]
                parts += [terms[1] * ys[m : m + 1] for m in range(3)]
                parts += [terms[2] * ys[m : m + 1] for m in range(3, 8)]
                sums = [p if s is None else s + p for s, p in zip(sums, parts)]
            for i in range(9):
                acc[i, rows[0], :] = sums[i]
            return carry

        lax.fori_loop(0, CHANNELS // CHUNK, chunk, 0)

    def interaction(t, feats):
        gather_sum(t)
        wide = acc[...].reshape(9 * 128, 128)
        wide = jnp.concatenate(halves(wide), axis=1).astype(BF16)
        moments = 0.25 * dot(select_wide, wide, NT)
        parts = [moments[:, 128 * i : 128 * i + 128] for i in range(9)]
        vector = parts[1] * parts[1] + parts[2] * parts[2] + parts[3] * parts[3]
        tensor = parts[4] * parts[4]
        for i in range(5, 9):
            tensor = tensor + parts[i] * parts[i]
        invariants = jnp.concatenate([parts[0], vector, tensor], axis=1)
        return feats + dot_split(invariants, mix_ref[t], NN), parts

    def interaction_back(t, grad, parts):
        inv_grad = dot_split(grad, mix_ref[t], NT)
        grads = [0.25 * inv_grad[:, 0:128]]
        grads += [0.5 * inv_grad[:, 128:256] * parts[i] for i in range(1, 4)]
        grads += [0.5 * inv_grad[:, 256:384] * parts[i] for i in range(4, 9)]
        deep = jnp.concatenate(grads, axis=1)
        deep = jnp.concatenate(halves(deep), axis=0).astype(BF16)
        expanded[...] = dot(deep, select_deep, TN).reshape(9, 128, 128)


    def source_back():
        def tile_back(k, carry):
            tile = lanes(k)
            ys = harm[k]
            for ci in range(CHANNELS // CHUNK):
                rows = [slice(128 * q + CHUNK * ci, 128 * q + CHUNK * ci + CHUNK) for q in range(3)]
                wide = [expanded[i, rows[0], :] for i in range(9)]
                pulls = [wide[0], wide[1] * ys[0:1], wide[4] * ys[3:4]]
                for m in range(1, 3):
                    pulls[1] = pulls[1] + wide[1 + m] * ys[m : m + 1]
                for m in range(4, 8):
                    pulls[2] = pulls[2] + wide[1 + m] * ys[m : m + 1]
                rads = [radial[1, rows[q], tile] for q in range(3)]
                high, low = halves(rads[0] * pulls[0] + rads[1] * pulls[1] + rads[2] * pulls[2])
                source_grad[rows[0], tile] = high.astype(BF16)
                source_grad[rows[1], tile] = low.astype(BF16)
            return carry

        lax.fori_loop(0, TILES, tile_back, 0)

    def edge_back(t):
        def tile_back(k, carry):
            tile = lanes(k)
            ys = harm[k]
            slopes = [jnp.zeros((8, 128), F32)] * 9
            sums = [jnp.zeros((8, 128), F32)] * 8
            for ci in range(CHANNELS // CHUNK):
                rows = [slice(128 * q + CHUNK * ci, 128 * q + CHUNK * ci + CHUNK) for q in range(3)]
                src = source[t, rows[0], tile]
                steep = [slope[t, rows[q], tile] * src for q in range(3)]
                terms = [term[t, rows[q], tile] for q in range(2)]
                for m in range(9):
                    wide = expanded[m, rows[0], :]
                    q = 0 if m < 1 else 1 if m < 4 else 2
                    value = wide * steep[q]
                    slopes[m] = slopes[m] + (value[0:8] + value[8:16])
                    if m > 0:
                        value = wide * terms[q - 1]
                        sums[m - 1] = sums[m - 1] + (value[0:8] + value[8:16])
            along = slopes[0]
            for m in range(8):
                along = along + slopes[1 + m] * ys[m : m + 1]
            tops = [jnp.sum(s, axis=0, keepdims=True) for s in sums + [along]]
            tops.append(jnp.zeros((7, 128), F32))
            edge_grad[t, k] = jnp.concatenate(tops, axis=0)
            return carry

        lax.fori_loop(0, TILES, tile_back, 0)

    radial[0] = radial_out(0, hidden)
    element = geo[3]
    for k in range(TILES):
        tile = slice(128 * k, 128 * k + 128)
        hot = (row.astype(F32) == element[k : k + 1]).astype(F32).astype(BF16)
        both = dot(emb_source, hot, NN)
        source[0, :, tile] = both[0:128] + both[128:256]
    h_one, parts_one = interaction(0, h_zero)

    mine[...] = dot_split(h_one, source_ref[1], NN)[0:ATOMS]
    second = [remote(1, b, mine, feat.at[b], minus(OFFSETS[b])) for b in OTHERS]
    for copy in second:
        copy.start()
    table[...] = jnp.zeros_like(table)
    table[OWN, 0:ATOMS] = mine[...]
    later_hidden = jnp.concatenate([later[...], later[...]], axis=0)
    radial[1] = radial_out(1, later_hidden)
    tilted = dsilu[...] * radial_in(jnp.concatenate([dbasis_ref[k] for k in range(TILES)], axis=1))
    slope[0] = radial_out(0, tilted)
    slope[1] = radial_out(1, tilted)
    for b, copy in zip(OTHERS[::-1], second[::-1]):
        copy.wait_recv()
        table[b, 0:ATOMS] = feat[b]

    turned = jnp.transpose(table[...].reshape(TABLE, 128))
    turned = jnp.concatenate(halves(turned), axis=0).astype(BF16)
    both = dot(turned, onehot[...], NN)
    source[1] = both[0:128] + both[128:256]
    h_two, parts_two = interaction(1, h_one)
    inner = dot_split(h_two, read_hidden_ref[...], NT)
    gate = 1.0 / (1.0 + jnp.exp(-inner))
    inner_grad = gate * (1.0 + inner * (1.0 - gate)) * read_two_ref[...]
    grad_two = dot_split(inner_grad, read_hidden_ref[...], NN)
    interaction_back(1, grad_two, parts_two)
    source_back()

    both = dot(onehot[...], source_grad[...], NT)
    both = both[:, 0:128] + both[:, 128:256]
    for b in range(27):
        feat_grad[b] = both[ROWS * b : ROWS * b + ATOMS]
    third_copies = [remote(2, b, feat_grad.at[b], feat_back.at[b], OFFSETS[b]) for b in OTHERS]
    for copy in third_copies:
        copy.start()
    edge_back(1)
    learned = jnp.sum(h_one * read_one_ref[...], axis=1, keepdims=True) + jnp.sum(
        inner * gate * read_two_ref[...], axis=1, keepdims=True
    )
    energy = jnp.sum((isolated + learned) * unsend[0:ROWS], axis=0, keepdims=True)
    energy_ref[0, 0] = energy[:, 0:ATOMS]
    total = feat_grad[OWN]
    for b, copy in zip(OTHERS[::-1], third_copies[::-1]):
        copy.wait_recv()
        total = total + feat_back[b]
    table[OWN, 0:ATOMS] = total
    grad_one = grad_two + read_one_ref[...] + dot_split(table[OWN], source_ref[1], NT)

    interaction_back(0, grad_one, parts_one)
    edge_back(0)

    pulls = [edge_grad[0, :, m, :] + edge_grad[1, :, m, :] for m in range(9)]
    along = pulls[8]
    gx = r3 * pulls[0] + r15 * (ny * pulls[3] + nz * pulls[6] + nx * pulls[7])
    gy = r3 * pulls[1] + r15 * (nx * pulls[3] + nz * pulls[4] - ny * pulls[7])
    gz = r3 * pulls[2] + r15 * (ny * pulls[4] + nx * pulls[6]) + 3.0 * r5 * nz * pulls[5]
    radially = along - (nx * gx + ny * gy + nz * gz) * inverse
    pulls = [radially * n + g * inverse for n, g in ((nx, gx), (ny, gy), (nz, gz))]
    highs = []
    for k in range(TILES):
        blocks = jnp.concatenate([bhot[k] * p[k : k + 1] for p in pulls], axis=0)
        highs.append(jnp.concatenate(halves(blocks), axis=0))
    blocks = jnp.concatenate(highs, axis=1).astype(BF16)
    both = dot(blocks, ghot[...], NT)
    both = both[0:96] + both[96:192]
    rows = both[0:32]
    for c in range(1, 3):
        rows = rows + pltpu.roll(both[32 * c : 32 * c + 32], 32 * c, 1)
    for b in range(27):
        leaving[b] = rows[b : b + 1]
    fourth = [
        remote(3, b, leaving.at[b], returned.at[b], OFFSETS[b]) for b in OTHERS
    ]
    for copy in fourth:
        copy.start()
    sums = [jnp.sum(p, axis=0, keepdims=True) for p in pulls] + [jnp.zeros((5, 128), F32)]
    force = pick(jnp.concatenate(sums, axis=0), spread, NT)
    own_row = rows[OWN : OWN + 1]
    force = force - jnp.concatenate([unrolled(own_row, c) for c in range(3)] + [sums[3]], axis=0)
    for copy in fourth:
        copy.wait_recv()
    back = returned[OTHERS[0]]
    for b in OTHERS[1:]:
        back = back + returned[b]
    back = jnp.concatenate([unrolled(back, c) for c in range(3)] + [sums[3]], axis=0)
    force = force - pick(back, unsend, NN)
    for c in range(3):
        force_ref[0, 0, c] = force[c : c + 1, 0:ATOMS]
    for copy in first + second + third_copies + fourth:
        copy.wait_send()


def per_device(
    positions,
    species,
    send_rows,
    neighbours,
    embedding,
    self_energy,
    source_weight,
    radial_in,
    radial_out,
    mix_weight,
    read_one,
    read_hidden,
    read_two,
):
    vmem = pl.BlockSpec(memory_space=pltpu.VMEM)
    hbm = pl.BlockSpec(memory_space=pltpu.HBM)
    energy, forces = pl.pallas_call(
        kernel,
        out_shape=(
            jax.ShapeDtypeStruct((1, 1, 1, ATOMS), F32),
            jax.ShapeDtypeStruct((1, 1, 3, 1, ATOMS), F32),
        ),
        in_specs=[vmem] * 4 + [hbm, vmem] + [hbm] * 4 + [vmem] * 3,
        out_specs=(vmem, vmem),
        scratch_shapes=[
            pltpu.VMEM(embedding.shape, F32),
            pltpu.VMEM(source_weight.shape, F32),
            pltpu.VMEM(radial_in.shape, F32),
            pltpu.VMEM(radial_out.shape, F32),
            pltpu.VMEM(mix_weight.shape, F32),
            pltpu.VMEM((16, 128), F32),
            pltpu.VMEM((128, 128), F32),
            pltpu.VMEM((136, 128), F32),
            pltpu.VMEM((1, 1, 128), F32),
            pltpu.VMEM((32, 1, 128), F32),
            pltpu.VMEM((27, 1, 128), F32),
            pltpu.VMEM((27, 1, 128), F32),
            pltpu.VMEM((ATOMS, 128), F32),
            pltpu.VMEM((27, ATOMS, 128), F32),
            pltpu.VMEM((28, ROWS, 128), F32),
            pltpu.VMEM((27, ATOMS, 128), F32),
            pltpu.VMEM((27, ATOMS, 128), F32),
            pltpu.VMEM((TABLE, EDGES), BF16),
            pltpu.VMEM((128, EDGES), BF16),
            pltpu.VMEM((TILES, 32, 128), F32),
            pltpu.VMEM((4, 8, 128), F32),
            pltpu.VMEM((TILES, ORDERS, 128), F32),
            pltpu.VMEM((TILES, ORDERS, 128), F32),
            pltpu.VMEM((TILES, 8, 128), F32),
            pltpu.VMEM((2, TILES, 16, 128), F32),
            pltpu.VMEM((2, 384, EDGES), F32),
            pltpu.VMEM((2, 384, EDGES), F32),
            pltpu.VMEM((2, 256, EDGES), F32),
            pltpu.VMEM((128, EDGES), F32),
            pltpu.VMEM((HIDDEN, EDGES), F32),
            pltpu.VMEM((2, 128, EDGES), F32),
            pltpu.VMEM((256, EDGES), BF16),
            pltpu.VMEM((9, 128, 128), F32),
            pltpu.VMEM((9, 128, 128), F32),
            pltpu.SemaphoreType.DMA((4, 27)),
            pltpu.SemaphoreType.DMA((4, 27)),
            pltpu.SemaphoreType.DMA((5,)),
        ],
        compiler_params=pltpu.CompilerParams(
            collective_id=0, has_side_effects=True, vmem_limit_bytes=55168 * 1024
        ),
        name="energy_and_forces",
    )(
        positions.transpose(0, 1, 3, 2, 4),
        species,
        send_rows,
        neighbours.transpose(0, 1, 4, 2, 3),
        embedding,
        self_energy[None],
        source_weight,
        radial_in,
        radial_out,
        mix_weight,
        read_one[None],
        read_hidden.T,
        read_two[None],
    )
    return energy, forces.transpose(0, 1, 3, 2, 4)


def solution(mesh):
    return jax.shard_map(
        per_device,
        mesh=mesh,
        in_specs=(
            P("gx", "gy", "gz", None, None),
            P("gx", "gy", "gz", None),
            P("gx", "gy", "gz", None),
            P("gx", "gy", "gz", None, None),
            P(),
            P(),
            P(),
            P(),
            P(),
            P(),
            P(),
            P(),
            P(),
        ),
        out_specs=(P("gx", "gy", "gz", None), P("gx", "gy", "gz", None, None)),
        check_vma=False,
    )
```

```python
import functools
import math

import jax
import jax.numpy as jnp
from jax import lax
from jax.experimental import pallas as pl
from jax.experimental.pallas import tpu as pltpu
from jax.sharding import PartitionSpec as P

F32 = jnp.float32
BF16 = jnp.bfloat16
HIGHEST = lax.Precision.HIGHEST
MESH = pl.DeviceIdType.MESH
CUTOFF = 6.0
BOX = (7.5, 7.5, 5.0)
ATOMS = 18
SLOTS = 56
CHANNELS = 128
HIDDEN = 64
ORDERS = 8
ROWS = 24
TABLE = 28 * ROWS
EDGES = 1024
TILES = 8
CHUNK = 16
OWN = 13
OFFSETS = tuple((b // 9 - 1, b // 3 % 3 - 1, b % 3 - 1) for b in range(27))
OTHERS = tuple(
    sorted(
        (b for b in range(27) if b != OWN),
        key=lambda b: -sum(abs(o) * w for o, w in zip(OFFSETS[b], (2, 1, 4))),
    )
)
NN = ((1,), (0,))
NT = ((1,), (1,))
TN = ((0,), (0,))


def dot(left, right, dims, precision=None):
    return lax.dot_general(
        left, right, (dims, ((), ())), precision=precision, preferred_element_type=F32
    )


def pick(value, selector, dims):
    high, low = halves(value)
    middle, low = halves(low)
    parts = jnp.concatenate([high, middle, low, jnp.zeros_like(low)], axis=0).astype(BF16)
    parts = dot(parts, selector.astype(BF16), dims)
    return (parts[0:8] + parts[8:16]) + parts[16:24]


def halves(value):
    high = value.astype(BF16).astype(F32)
    return high, value - high


def dot_split(left, right, dims):
    left_high, left_low = halves(left)
    right_high, right_low = halves(right)
    left_high = left_high.astype(BF16)
    right_high = right_high.astype(BF16)
    return (
        dot(left_high, right_high, dims)
        + dot(left_high, right_low.astype(BF16), dims)
        + dot(left_low.astype(BF16), right_high, dims)
    )


def parted(value, axis):
    return jnp.concatenate(halves(value), axis=axis).astype(BF16)


def apply(left, right, dims):
    both = dot(parted(left, 0), right, dims)
    both = both[0:ROWS] + both[ROWS : 2 * ROWS]
    half = both.shape[1] // 2
    return both[:, 0:half] + both[:, half:]


def iota(shape, dim):
    return lax.broadcasted_iota(jnp.int32, shape, dim)


def over(value, divisor):
    return (value * (65536 // divisor + 1)) >> 16


def lanes(index):
    return pl.ds(pl.multiple_of(index * 128, 128), 128)


def column(row, rows):
    return jnp.transpose(jnp.broadcast_to(row, (128, 128)))[0:rows]


def packed(values):
    row = values[0:1]
    for c in range(1, 4):
        row = row + pltpu.roll(values[c : c + 1], 32 * c, 1)
    return row


def unrolled(values, c):
    return values if c == 0 else pltpu.roll(values, 128 - 32 * c, 1)


def kernel(
    pos_hbm,
    species_hbm,
    send_hbm,
    nbr_hbm,
    emb_hbm,
    self_hbm,
    source_hbm,
    rin_hbm,
    rout_hbm,
    mix_hbm,
    read_one_hbm,
    read_hidden_hbm,
    read_two_hbm,
    energy_ref,
    force_ref,
    pos_ref,
    species_ref,
    send_ref,
    nbr_ref,
    emb_ref,
    self_ref,
    source_ref,
    rin_ref,
    rout_ref,
    mix_ref,
    read_one_ref,
    read_hidden_ref,
    read_two_ref,
    stage,
    slots,
    table_emb,
    packet,
    arrived,
    leaving,
    returned,
    mine,
    feat,
    table,
    feat_grad,
    feat_back,
    onehot,
    ghot,
    gdeep,
    bhot,
    geo,
    basis_ref,
    dbasis_ref,
    harm,
    edge_grad,
    radial,
    slope,
    term,
    dsilu,
    later,
    source,
    source_grad,
    acc,
    expanded,
    sent,
    received,
    loaded,
):
    me = (lax.axis_index("gx"), lax.axis_index("gy"), lax.axis_index("gz"))
    extent = (3, 16, 16)

    def device(offset):
        return tuple(lax.rem(m + (o + n), n) for m, o, n in zip(me, offset, extent))

    def minus(offset):
        return tuple(-o for o in offset)

    inputs = [
        pltpu.make_async_copy(src, dst, loaded.at[i])
        for i, (src, dst) in enumerate(
            (
                (pos_hbm, pos_ref),
                (species_hbm, species_ref),
                (send_hbm, send_ref),
                (nbr_hbm, nbr_ref),
                (emb_hbm, emb_ref),
                (self_hbm, self_ref),
                (source_hbm, source_ref),
                (rin_hbm, rin_ref),
                (rout_hbm, rout_ref),
                (mix_hbm, mix_ref),
                (read_one_hbm, read_one_ref),
                (read_hidden_hbm, read_hidden_ref),
                (read_two_hbm, read_two_ref),
            )
        )
    ]
    for copy in inputs[0:3]:
        copy.start()
    barrier = pltpu.get_barrier_semaphore()
    for b in OTHERS:
        pl.semaphore_signal(barrier, inc=1, device_id=device(OFFSETS[b]), device_id_type=MESH)
    for copy in inputs[3:]:
        copy.start()

    def remote(phase, index, src, dst, offset):
        return pltpu.make_async_remote_copy(
            src_ref=src,
            dst_ref=dst,
            send_sem=sent.at[phase, index],
            recv_sem=received.at[phase, index],
            device_id=device(offset),
            device_id_type=MESH,
        )

    stage[...] = jnp.zeros_like(stage)
    for copy in inputs[0:3]:
        copy.wait()
    for c in range(3):
        stage[c : c + 1, 0:ATOMS] = pos_ref[0, 0, c]
    stage[3:4, 0:ATOMS] = species_ref[0, 0].astype(F32)
    stage[8:9, 0:ATOMS] = send_ref[0, 0].astype(F32)
    lane = iota((128, 128), 1)
    row = iota((128, 128), 0)
    send_row = jnp.where(lane[0:1] < ATOMS, stage[8:9], -5.0)
    own = stage[0:8]
    to_send = (row.astype(F32) == send_row).astype(F32)
    own_send = pick(own, to_send, NN)
    packet[0] = packed(own_send)
    arrived[OWN] = packed(own)
    arrived[27:32] = jnp.zeros((5, 1, 128), F32)
    pl.semaphore_wait(barrier, 26)
    first = [
        remote(0, b, packet.at[0], arrived.at[b], minus(OFFSETS[b])) for b in OTHERS
    ]
    for copy in first:
        copy.start()

    send_col = column(send_row, 128)
    lane_atom = jnp.where(lane < 7 * ATOMS, lane - ATOMS * over(lane, ATOMS), -7)
    select = (send_col[0:ROWS] == lane_atom[0:ROWS].astype(F32)).astype(F32)
    select_wide = jnp.concatenate([select, select], axis=1).astype(BF16)
    select_deep = jnp.concatenate([select, select], axis=0).astype(BF16)
    unsend = (send_col == lane.astype(F32)).astype(F32)
    spread = (row == lane_atom).astype(F32)
    centre = pick(own, spread, NN)

    slots[...] = jnp.zeros_like(slots)
    inputs[3].wait()
    for a in range(ATOMS):
        slots[a : a + 1, 0:SLOTS] = (nbr_ref[0, 0, a] + 1).astype(F32)
    by_slot = jnp.transpose(slots[...])
    named = by_slot[0:8]
    for j in range(1, 7):
        named = named + pltpu.roll(by_slot[8 * j : 8 * j + 8], ATOMS * j, 1)
    named = named.astype(jnp.int32) - 1
    outer = jnp.maximum(named - ATOMS, 0)
    block = jnp.where(named < 0, -1, jnp.where(named < ATOMS, OWN, over(outer, ATOMS)))
    member = jnp.where(named < ATOMS, named, outer - ATOMS * over(outer, ATOMS))
    usable = (named >= 0).astype(F32)

    table_row = iota((TABLE, 128), 0)
    table_block = over(table_row, ROWS)
    table_member = table_row - ROWS * table_block
    label = jnp.where(
        (table_member < ATOMS) & (table_block < 27),
        ATOMS + ATOMS * table_block + table_member,
        -2,
    )
    label = jnp.concatenate(
        [label[0 : OWN * ROWS], send_col[0:ROWS].astype(jnp.int32), label[(OWN + 1) * ROWS :]],
        axis=0,
    )
    for k in range(TILES):
        tile = slice(128 * k, 128 * k + 128)
        onehot[:, tile] = (label == named[k : k + 1]).astype(F32).astype(BF16)
        ghot[:, tile] = (row == member[k : k + 1]).astype(F32).astype(BF16)
        bhot[k] = (row[0:32] == block[k : k + 1]).astype(F32)

    table_emb[...] = jnp.zeros_like(table_emb)
    for copy in inputs[4:]:
        copy.wait()
    table_emb[0:89] = emb_ref[...]
    table_emb[128:129, 0:89] = self_ref[...]
    embedding = table_emb[0:128]
    species_col = column(own_send[3:4], ROWS)
    own_hot = (
        (species_col == lane[0:ROWS].astype(F32)) & (row[0:ROWS] < ATOMS)
    ).astype(F32)
    h_zero = dot(own_hot, embedding, NN, HIGHEST)
    isolated = jnp.sum(own_hot * table_emb[128:129], axis=1, keepdims=True)
    emb_source = dot_split(jnp.transpose(source_ref[0]), embedding, NT)
    emb_source = jnp.concatenate(halves(emb_source), axis=0).astype(BF16)

    rin_high, rin_low = halves(jnp.concatenate([rin_ref[0], rin_ref[1]], axis=1))
    rin_wide = jnp.concatenate(
        [rin_high, rin_high, rin_low, jnp.zeros((104, 128), F32)], axis=0
    )
    rin_wide = jnp.transpose(rin_wide)[:, 0:32].astype(BF16)
    rout_wide = []
    for t in range(2):
        high, low = halves(rout_ref[t])
        rout_wide.append(
            jnp.transpose(jnp.concatenate([high, high, low, low], axis=0)).astype(BF16)
        )

    read_hidden = read_hidden_ref[...]
    chain = dot_split(mix_ref[0], source_ref[1], NN)
    chain_wide = parted(chain, 1)
    chain_deep = parted(chain, 0)
    read_in = parted(dot_split(mix_ref[1], read_hidden, NT), 1)
    read_out = parted(dot_split(read_hidden, mix_ref[1], NT), 1)
    zero_source = dot_split(h_zero, source_ref[1], NN)
    for k in range(TILES):
        tile = slice(128 * k, 128 * k + 128)
        repeated = jnp.where(row < 96, row - 32 * over(row, 32), -3)
        gdeep[:, tile] = (repeated == member[k : k + 1]).astype(F32).astype(BF16)

    for copy in first:
        copy.wait_recv()
    lane_part = over(lane[0:32], 32)
    domain = row[0:32]
    third = over(domain, 3)
    shift = jnp.where(
        lane_part == 0,
        (over(domain, 9) - 1).astype(F32) * BOX[0],
        jnp.where(
            lane_part == 1,
            (third - 3 * over(domain, 9) - 1).astype(F32) * BOX[1],
            jnp.where(lane_part == 2, (domain - 3 * third - 1).astype(F32) * BOX[2], 0.0),
        ),
    )
    nearby = arrived[...].reshape(32, 128) + shift
    nearby = jnp.concatenate([unrolled(nearby, c) for c in range(4)], axis=0)
    high, low = halves(jnp.where(lane < 32, nearby, 0.0))
    middle, low = halves(low)
    nearby = high + pltpu.roll(middle, 32, 1) + pltpu.roll(low, 64, 1)
    by_block = dot(nearby.astype(BF16), gdeep[...], NN)
    for k in range(TILES):
        tile = slice(128 * k, 128 * k + 128)
        for c in range(4):
            geo[c, k : k + 1, :] = jnp.sum(
                by_block[32 * c : 32 * c + 32, tile] * bhot[k], axis=0, keepdims=True
            )

    dx = geo[0] - centre[0:1]
    dy = geo[1] - centre[1:2]
    dz = geo[2] - centre[2:3]
    distance = jnp.sqrt(dx * dx + dy * dy + dz * dz + 0.25)
    inverse = 1.0 / distance
    nx = dx * inverse
    ny = dy * inverse
    nz = dz * inverse
    scaled = jnp.minimum(distance * (1.0 / CUTOFF), 1.0)
    square = scaled * scaled
    fifth = square * square * scaled
    sixth = fifth * scaled
    seventh = sixth * scaled
    envelope = 1.0 - 28.0 * sixth + 48.0 * seventh - 21.0 * seventh * scaled
    envelope_grad = (-168.0 * fifth + 336.0 * sixth - 168.0 * seventh) * (1.0 / CUTOFF)
    weight = math.sqrt(2.0 / CUTOFF) * inverse * usable
    weight_grad = weight * (envelope_grad - envelope * inverse)
    weight = weight * envelope
    angle = distance * (math.pi / CUTOFF)
    sine_one = jnp.sin(angle)
    cosine_one = jnp.cos(angle)
    sine, cosine = sine_one, cosine_one
    sine_last, cosine_last = jnp.zeros_like(angle), jnp.ones_like(angle)
    for m in range(ORDERS):
        basis_ref[:, m, :] = weight * sine
        dbasis_ref[:, m, :] = weight_grad * sine + weight * cosine * ((m + 1) * math.pi / CUTOFF)
        sine, sine_last = 2.0 * cosine_one * sine - sine_last, sine
        cosine, cosine_last = 2.0 * cosine_one * cosine - cosine_last, cosine
    r3, r5, r15 = math.sqrt(3.0), math.sqrt(5.0), math.sqrt(15.0)
    for m, value in enumerate(
        (
            r3 * nx,
            r3 * ny,
            r3 * nz,
            r15 * nx * ny,
            r15 * ny * nz,
            0.5 * r5 * (3.0 * nz * nz - 1.0),
            r15 * nx * nz,
            0.5 * r15 * (nx * nx - ny * ny),
        )
    ):
        harm[:, m, :] = value

    basis = jnp.concatenate([basis_ref[k] for k in range(TILES)], axis=1)

    def radial_in(value):
        high, low = halves(value)
        value = jnp.concatenate([high, low, high, jnp.zeros_like(high)], axis=0).astype(BF16)
        return dot(rin_wide, value, NN)

    pre = radial_in(basis)
    gate = 1.0 / (1.0 + jnp.exp(-pre))
    hidden = pre * gate
    dsilu[...] = gate * (1.0 + pre * (1.0 - gate))
    later[...] = hidden[HIDDEN : 2 * HIDDEN]

    def radial_out(t, value):
        high, low = halves(value[HIDDEN * t : HIDDEN * t + HIDDEN])
        deep = jnp.concatenate([high, low, high, low], axis=0).astype(BF16)
        return dot(rout_wide[t], deep, NN)

    def gather_sum(t):
        def chunk(ci, carry):
            c0 = pl.multiple_of(ci * CHUNK, CHUNK)
            rows = [pl.ds(pl.multiple_of(128 * q + c0, CHUNK), CHUNK) for q in range(3)]
            sums = [None] * 9
            for k in range(TILES):
                tile = slice(128 * k, 128 * k + 128)
                src = source[t, rows[0], tile]
                terms = [radial[t, rows[q], tile] * src for q in range(3)]
                term[t, rows[0], tile] = terms[1]
                term[t, rows[1], tile] = terms[2]
                ys = harm[k]
                parts = [terms[0]]
                parts += [terms[1] * ys[m : m + 1] for m in range(3)]
                parts += [terms[2] * ys[m : m + 1] for m in range(3, 8)]
                sums = [p if s is None else s + p for s, p in zip(sums, parts)]
            for i in range(9):
                acc[i, rows[0], :] = sums[i]
            return carry

        lax.fori_loop(0, CHANNELS // CHUNK, chunk, 0)

    def interaction(t):
        gather_sum(t)
        wide = acc[...].reshape(9 * 128, 128)
        wide = jnp.concatenate(halves(wide), axis=1).astype(BF16)
        moments = 0.25 * dot(select_wide, wide, NT)
        parts = [moments[:, 128 * i : 128 * i + 128] for i in range(9)]
        vector = parts[1] * parts[1] + parts[2] * parts[2] + parts[3] * parts[3]
        tensor = parts[4] * parts[4]
        for i in range(5, 9):
            tensor = tensor + parts[i] * parts[i]
        return jnp.concatenate([parts[0], vector, tensor], axis=1), parts

    def interaction_back(inv_grad, parts):
        grads = [0.25 * inv_grad[:, 0:128]]
        grads += [0.5 * inv_grad[:, 128:256] * parts[i] for i in range(1, 4)]
        grads += [0.5 * inv_grad[:, 256:384] * parts[i] for i in range(4, 9)]
        deep = jnp.concatenate(grads, axis=1)
        deep = jnp.concatenate(halves(deep), axis=0).astype(BF16)
        expanded[...] = dot(deep, select_deep, TN).reshape(9, 128, 128)

    def source_back():
        def tile_back(k, carry):
            tile = lanes(k)
            ys = harm[k]
            for ci in range(CHANNELS // CHUNK):
                rows = [slice(128 * q + CHUNK * ci, 128 * q + CHUNK * ci + CHUNK) for q in range(3)]
                wide = [expanded[i, rows[0], :] for i in range(9)]
                pulls = [wide[0], wide[1] * ys[0:1], wide[4] * ys[3:4]]
                for m in range(1, 3):
                    pulls[1] = pulls[1] + wide[1 + m] * ys[m : m + 1]
                for m in range(4, 8):
                    pulls[2] = pulls[2] + wide[1 + m] * ys[m : m + 1]
                rads = [radial[1, rows[q], tile] for q in range(3)]
                high, low = halves(rads[0] * pulls[0] + rads[1] * pulls[1] + rads[2] * pulls[2])
                source_grad[rows[0], tile] = high.astype(BF16)
                source_grad[rows[1], tile] = low.astype(BF16)
            return carry

        lax.fori_loop(0, TILES, tile_back, 0)

    def edge_back(t):
        def tile_back(k, carry):
            tile = lanes(k)
            ys = harm[k]
            slopes = [jnp.zeros((8, 128), F32)] * 9
            sums = [jnp.zeros((8, 128), F32)] * 8
            for ci in range(CHANNELS // CHUNK):
                rows = [slice(128 * q + CHUNK * ci, 128 * q + CHUNK * ci + CHUNK) for q in range(3)]
                src = source[t, rows[0], tile]
                steep = [slope[t, rows[q], tile] for q in range(3)]
                if t == 1:
                    steep = [value * src for value in steep]
                terms = [term[t, rows[q], tile] for q in range(2)]
                for m in range(9):
                    wide = expanded[m, rows[0], :]
                    q = 0 if m < 1 else 1 if m < 4 else 2
                    value = wide * steep[q]
                    slopes[m] = slopes[m] + (value[0:8] + value[8:16])
                    if m > 0:
                        value = wide * terms[q - 1]
                        sums[m - 1] = sums[m - 1] + (value[0:8] + value[8:16])
            along = slopes[0]
            for m in range(8):
                along = along + slopes[1 + m] * ys[m : m + 1]
            tops = [jnp.sum(s, axis=0, keepdims=True) for s in sums + [along]]
            tops.append(jnp.zeros((7, 128), F32))
            edge_grad[t, k] = jnp.concatenate(tops, axis=0)
            return carry

        lax.fori_loop(0, TILES, tile_back, 0)

    radial[0] = radial_out(0, hidden)
    element = geo[3]
    for k in range(TILES):
        tile = slice(128 * k, 128 * k + 128)
        hot = (row.astype(F32) == element[k : k + 1]).astype(F32).astype(BF16)
        both = dot(emb_source, hot, NN)
        source[0, :, tile] = both[0:128] + both[128:256]
    invariants, parts_one = interaction(0)

    mine[...] = (zero_source + apply(invariants, chain_wide, NN))[0:ATOMS]
    second = [remote(1, b, mine, feat.at[b], minus(OFFSETS[b])) for b in OTHERS]
    for copy in second:
        copy.start()
    table[...] = jnp.zeros_like(table)
    table[OWN, 0:ATOMS] = mine[...]
    h_one = h_zero + dot_split(invariants, mix_ref[0], NN)
    read_one = dot_split(h_one, read_hidden, NT)
    later_hidden = jnp.concatenate([later[...], later[...]], axis=0)
    radial[1] = radial_out(1, later_hidden)
    tilted = dsilu[...] * radial_in(jnp.concatenate([dbasis_ref[k] for k in range(TILES)], axis=1))
    steep = radial_out(0, tilted)
    for q in range(3):
        slope[0, 128 * q : 128 * q + 128] = steep[128 * q : 128 * q + 128] * source[0]
    slope[1] = radial_out(1, tilted)
    for b, copy in zip(OTHERS[::-1], second[::-1]):
        copy.wait_recv()
        table[b, 0:ATOMS] = feat[b]

    turned = jnp.transpose(table[...].reshape(TABLE, 128))
    turned = jnp.concatenate(halves(turned), axis=0).astype(BF16)
    both = dot(turned, onehot[...], NN)
    source[1] = both[0:128] + both[128:256]
    invariants, parts_two = interaction(1)
    inner = read_one + apply(invariants, read_in, NN)
    gate = 1.0 / (1.0 + jnp.exp(-inner))
    inner_grad = gate * (1.0 + inner * (1.0 - gate)) * read_two_ref[...]
    interaction_back(apply(inner_grad, read_out, NN), parts_two)
    source_back()

    both = dot(onehot[...], source_grad[...], NT)
    both = both[:, 0:128] + both[:, 128:256]
    for b in range(27):
        feat_grad[b] = both[ROWS * b : ROWS * b + ATOMS]
    third_copies = [remote(2, b, feat_grad.at[b], feat_back.at[b], OFFSETS[b]) for b in OTHERS]
    for copy in third_copies:
        copy.start()
    grad_two = dot_split(inner_grad, read_hidden, NN) + read_one_ref[...]
    grad_two = dot_split(grad_two, mix_ref[0], NT)
    edge_back(1)
    learned = jnp.sum(h_one * read_one_ref[...], axis=1, keepdims=True) + jnp.sum(
        inner * gate * read_two_ref[...], axis=1, keepdims=True
    )
    energy = jnp.sum((isolated + learned) * unsend[0:ROWS], axis=0, keepdims=True)
    energy_ref[0, 0] = -energy[:, 0:ATOMS]
    total = feat_grad[OWN]
    for b, copy in zip(OTHERS[::-1], third_copies[::-1]):
        copy.wait_recv()
        total = total + feat_back[b]
    table[OWN, 0:ATOMS] = total
    grad_one = grad_two + apply(table[OWN], chain_deep, NT)

    interaction_back(grad_one, parts_one)
    edge_back(0)

    pulls = [edge_grad[0, :, m, :] + edge_grad[1, :, m, :] for m in range(9)]
    along = pulls[8]
    gx = r3 * pulls[0] + r15 * (ny * pulls[3] + nz * pulls[6] + nx * pulls[7])
    gy = r3 * pulls[1] + r15 * (nx * pulls[3] + nz * pulls[4] - ny * pulls[7])
    gz = r3 * pulls[2] + r15 * (ny * pulls[4] + nx * pulls[6]) + 3.0 * r5 * nz * pulls[5]
    radially = along - (nx * gx + ny * gy + nz * gz) * inverse
    pulls = [radially * n + g * inverse for n, g in ((nx, gx), (ny, gy), (nz, gz))]
    highs = []
    for k in range(TILES):
        blocks = jnp.concatenate([bhot[k] * p[k : k + 1] for p in pulls], axis=0)
        highs.append(jnp.concatenate(halves(blocks), axis=0))
    blocks = jnp.concatenate(highs, axis=1).astype(BF16)
    both = dot(blocks, ghot[...], NT)
    both = both[0:96] + both[96:192]
    rows = both[0:32]
    for c in range(1, 3):
        rows = rows + pltpu.roll(both[32 * c : 32 * c + 32], 32 * c, 1)
    for b in range(27):
        leaving[b] = rows[b : b + 1]
    fourth = [
        remote(3, b, leaving.at[b], returned.at[b], OFFSETS[b]) for b in OTHERS
    ]
    for copy in fourth:
        copy.start()
    sums = [jnp.sum(p, axis=0, keepdims=True) for p in pulls] + [jnp.zeros((5, 128), F32)]
    force = pick(jnp.concatenate(sums, axis=0), spread, NT)
    own_row = rows[OWN : OWN + 1]
    force = jnp.concatenate([unrolled(own_row, c) for c in range(3)] + [sums[3]], axis=0) - force
    for copy in fourth:
        copy.wait_recv()
    back = returned[OTHERS[0]]
    for b in OTHERS[1:]:
        back = back + returned[b]
    back = jnp.concatenate([unrolled(back, c) for c in range(3)] + [sums[3]], axis=0)
    force = force + pick(back, unsend, NN)
    for c in range(3):
        force_ref[0, 0, c] = force[c : c + 1, 0:ATOMS]
    for copy in first + second + third_copies + fourth:
        copy.wait_send()


def per_device(
    positions,
    species,
    send_rows,
    neighbours,
    embedding,
    self_energy,
    source_weight,
    radial_in,
    radial_out,
    mix_weight,
    read_one,
    read_hidden,
    read_two,
):
    vmem = pl.BlockSpec(memory_space=pltpu.VMEM)
    energy, forces = pl.pallas_call(
        kernel,
        out_shape=(
            jax.ShapeDtypeStruct((1, 1, 1, ATOMS), F32),
            jax.ShapeDtypeStruct((1, 1, 3, 1, ATOMS), F32),
        ),
        in_specs=[pl.BlockSpec(memory_space=pltpu.HBM)] * 13,
        out_specs=(vmem, vmem),
        scratch_shapes=[
            pltpu.VMEM((1, 1, 3, 1, ATOMS), F32),
            pltpu.VMEM((1, 1, 1, ATOMS), jnp.int32),
            pltpu.VMEM((1, 1, 1, ATOMS), jnp.int32),
            pltpu.VMEM((1, 1, ATOMS, 1, SLOTS), jnp.int32),
            pltpu.VMEM(embedding.shape, F32),
            pltpu.VMEM((1, 89), F32),
            pltpu.VMEM(source_weight.shape, F32),
            pltpu.VMEM(radial_in.shape, F32),
            pltpu.VMEM(radial_out.shape, F32),
            pltpu.VMEM(mix_weight.shape, F32),
            pltpu.VMEM((1, 128), F32),
            pltpu.VMEM((16, 128), F32),
            pltpu.VMEM((1, 16), F32),
            pltpu.VMEM((16, 128), F32),
            pltpu.VMEM((128, 128), F32),
            pltpu.VMEM((136, 128), F32),
            pltpu.VMEM((1, 1, 128), F32),
            pltpu.VMEM((32, 1, 128), F32),
            pltpu.VMEM((27, 1, 128), F32),
            pltpu.VMEM((27, 1, 128), F32),
            pltpu.VMEM((ATOMS, 128), F32),
            pltpu.VMEM((27, ATOMS, 128), F32),
            pltpu.VMEM((28, ROWS, 128), F32),
            pltpu.VMEM((27, ATOMS, 128), F32),
            pltpu.VMEM((27, ATOMS, 128), F32),
            pltpu.VMEM((TABLE, EDGES), BF16),
            pltpu.VMEM((128, EDGES), BF16),
            pltpu.VMEM((128, EDGES), BF16),
            pltpu.VMEM((TILES, 32, 128), F32),
            pltpu.VMEM((4, 8, 128), F32),
            pltpu.VMEM((TILES, ORDERS, 128), F32),
            pltpu.VMEM((TILES, ORDERS, 128), F32),
            pltpu.VMEM((TILES, 8, 128), F32),
            pltpu.VMEM((2, TILES, 16, 128), F32),
            pltpu.VMEM((2, 384, EDGES), F32),
            pltpu.VMEM((2, 384, EDGES), F32),
            pltpu.VMEM((2, 256, EDGES), F32),
            pltpu.VMEM((128, EDGES), F32),
            pltpu.VMEM((HIDDEN, EDGES), F32),
            pltpu.VMEM((2, 128, EDGES), F32),
            pltpu.VMEM((256, EDGES), BF16),
            pltpu.VMEM((9, 128, 128), F32),
            pltpu.VMEM((9, 128, 128), F32),
            pltpu.SemaphoreType.DMA((4, 27)),
            pltpu.SemaphoreType.DMA((4, 27)),
            pltpu.SemaphoreType.DMA((13,)),
        ],
        compiler_params=pltpu.CompilerParams(
            collective_id=0, has_side_effects=True, vmem_limit_bytes=60 * 1024 * 1024
        ),
        name="energy_and_forces",
    )(
        positions.transpose(0, 1, 3, 2, 4),
        species,
        send_rows,
        neighbours.transpose(0, 1, 4, 2, 3),
        embedding,
        self_energy[None],
        source_weight,
        radial_in,
        radial_out,
        mix_weight,
        read_one[None],
        read_hidden.T,
        read_two[None],
    )
    return -energy, -forces.transpose(0, 1, 3, 2, 4)


def solution(mesh):
    return jax.shard_map(
        per_device,
        mesh=mesh,
        in_specs=(
            P("gx", "gy", "gz", None, None),
            P("gx", "gy", "gz", None),
            P("gx", "gy", "gz", None),
            P("gx", "gy", "gz", None, None),
            P(),
            P(),
            P(),
            P(),
            P(),
            P(),
            P(),
            P(),
            P(),
        ),
        out_specs=(P("gx", "gy", "gz", None), P("gx", "gy", "gz", None, None)),
        check_vma=False,
    )
```

```python
import functools
import math

import jax
import jax.numpy as jnp
from jax import lax
from jax.experimental import pallas as pl
from jax.experimental.pallas import tpu as pltpu
from jax.sharding import PartitionSpec as P

F32 = jnp.float32
BF16 = jnp.bfloat16
HIGHEST = lax.Precision.HIGHEST
MESH = pl.DeviceIdType.MESH
CUTOFF = 6.0
BOX = (7.5, 7.5, 5.0)
ATOMS = 18
SLOTS = 56
CHANNELS = 128
HIDDEN = 64
ORDERS = 8
ROWS = 24
GROUP = 256
EDGES = 1024
TILES = 8
CHUNK = 16
OWN = 13
OFFSETS = tuple((b // 9 - 1, b // 3 % 3 - 1, b % 3 - 1) for b in range(27))
OTHERS = tuple(
    sorted(
        (b for b in range(27) if b != OWN),
        key=lambda b: -sum(abs(o) * w for o, w in zip(OFFSETS[b], (2, 1, 4))),
    )
)
PLACES = (0, 1, 2, 3, 5, 6, 7, 8)
NN = ((1,), (0,))
NT = ((1,), (1,))
TN = ((0,), (0,))


def dot(left, right, dims, precision=None):
    return lax.dot_general(
        left, right, (dims, ((), ())), precision=precision, preferred_element_type=F32
    )


def pick(value, selector, dims):
    high, low = halves(value)
    middle, low = halves(low)
    parts = jnp.concatenate([high, middle, low, jnp.zeros_like(low)], axis=0).astype(BF16)
    parts = dot(parts, selector.astype(BF16), dims)
    return (parts[0:8] + parts[8:16]) + parts[16:24]


def halves(value):
    high = value.astype(BF16).astype(F32)
    return high, value - high


def dot_split(left, right, dims):
    left_high, left_low = halves(left)
    right_high, right_low = halves(right)
    left_high = left_high.astype(BF16)
    right_high = right_high.astype(BF16)
    return (
        dot(left_high, right_high, dims)
        + dot(left_high, right_low.astype(BF16), dims)
        + dot(left_low.astype(BF16), right_high, dims)
    )


def parted(value, axis):
    return jnp.concatenate(halves(value), axis=axis).astype(BF16)


def apply(left, right, dims):
    both = dot(parted(left, 0), right, dims)
    both = both[0:ROWS] + both[ROWS : 2 * ROWS]
    half = both.shape[1] // 2
    return both[:, 0:half] + both[:, half:]


def iota(shape, dim):
    return lax.broadcasted_iota(jnp.int32, shape, dim)


def over(value, divisor):
    return (value * (65536 // divisor + 1)) >> 16


def lanes(index):
    return pl.ds(pl.multiple_of(index * 128, 128), 128)


def column(row, rows):
    return jnp.transpose(jnp.broadcast_to(row, (128, 128)))[0:rows]


def packed(values):
    row = values[0:1]
    for c in range(1, 4):
        row = row + pltpu.roll(values[c : c + 1], 32 * c, 1)
    return row


def unrolled(values, c):
    return values if c == 0 else pltpu.roll(values, 128 - 32 * c, 1)


def kernel(
    pos_hbm,
    species_hbm,
    send_hbm,
    nbr_hbm,
    emb_hbm,
    self_hbm,
    source_hbm,
    rin_hbm,
    rout_hbm,
    mix_hbm,
    read_one_hbm,
    read_hidden_hbm,
    read_two_hbm,
    energy_ref,
    force_ref,
    pos_ref,
    species_ref,
    send_ref,
    nbr_ref,
    emb_ref,
    self_ref,
    source_ref,
    rin_ref,
    rout_ref,
    mix_ref,
    read_one_ref,
    read_hidden_ref,
    read_two_ref,
    stage,
    slots,
    table_emb,
    packet,
    arrived,
    leaving,
    returned,
    mine,
    feat,
    table,
    feat_grad,
    feat_back,
    onehot,
    ghot,
    gdeep,
    bhot,
    geo,
    basis_ref,
    dbasis_ref,
    harm,
    edge_grad,
    radial,
    slope,
    term,
    dsilu,
    later,
    source,
    source_grad,
    acc,
    expanded,
    sent,
    received,
    loaded,
):
    me = (lax.axis_index("gx"), lax.axis_index("gy"), lax.axis_index("gz"))
    extent = (3, 16, 16)

    def device(offset):
        return tuple(lax.rem(m + (o + n), n) for m, o, n in zip(me, offset, extent))

    def minus(offset):
        return tuple(-o for o in offset)

    inputs = [
        pltpu.make_async_copy(src, dst, loaded.at[i])
        for i, (src, dst) in enumerate(
            (
                (pos_hbm, pos_ref),
                (species_hbm, species_ref),
                (send_hbm, send_ref),
                (nbr_hbm, nbr_ref),
                (emb_hbm, emb_ref),
                (self_hbm, self_ref),
                (source_hbm, source_ref),
                (rin_hbm, rin_ref),
                (rout_hbm, rout_ref),
                (mix_hbm, mix_ref),
                (read_one_hbm, read_one_ref),
                (read_hidden_hbm, read_hidden_ref),
                (read_two_hbm, read_two_ref),
            )
        )
    ]
    for copy in inputs[0:3]:
        copy.start()
    barrier = pltpu.get_barrier_semaphore()
    for b in OTHERS:
        pl.semaphore_signal(barrier, inc=1, device_id=device(OFFSETS[b]), device_id_type=MESH)
    for copy in inputs[3:]:
        copy.start()

    across = jnp.where(lax.rem(me[2], 4) < 2, -1, 1)

    def remote(phase, index, src, dst, offset):
        return pltpu.make_async_remote_copy(
            src_ref=src,
            dst_ref=dst,
            send_sem=sent.at[phase, index],
            recv_sem=received.at[phase, index],
            device_id=device(offset),
            device_id_type=MESH,
        )

    stage[...] = jnp.zeros_like(stage)
    for copy in inputs[0:3]:
        copy.wait()
    for c in range(3):
        stage[c : c + 1, 0:ATOMS] = pos_ref[0, 0, c]
    stage[3:4, 0:ATOMS] = species_ref[0, 0].astype(F32)
    stage[8:9, 0:ATOMS] = send_ref[0, 0].astype(F32)
    lane = iota((128, 128), 1)
    row = iota((128, 128), 0)
    send_row = jnp.where(lane[0:1] < ATOMS, stage[8:9], -5.0)
    own = stage[0:8]
    to_send = (row.astype(F32) == send_row).astype(F32)
    own_send = pick(own, to_send, NN)
    packet[0] = packed(own_send)
    arrived[OWN] = packed(own)
    arrived[27:32] = jnp.zeros((5, 1, 128), F32)
    pl.semaphore_wait(barrier, 26)
    first = [
        remote(0, b, packet.at[0], arrived.at[b], minus(OFFSETS[b])) for b in OTHERS
    ]
    for copy in first:
        copy.start()

    send_col = column(send_row, 128)
    lane_atom = jnp.where(lane < 7 * ATOMS, lane - ATOMS * over(lane, ATOMS), -7)
    select = (send_col[0:ROWS] == lane_atom[0:ROWS].astype(F32)).astype(F32)
    select_wide = jnp.concatenate([select, select], axis=1).astype(BF16)
    select_deep = jnp.concatenate([select, select], axis=0).astype(BF16)
    unsend = (send_col == lane.astype(F32)).astype(F32)
    spread = (row == lane_atom).astype(F32)
    centre = pick(own, spread, NN)

    slots[...] = jnp.zeros_like(slots)
    inputs[3].wait()
    for a in range(ATOMS):
        slots[a : a + 1, 0:SLOTS] = (nbr_ref[0, 0, a] + 1).astype(F32)
    by_slot = jnp.transpose(slots[...])
    named = by_slot[0:8]
    for j in range(1, 7):
        named = named + pltpu.roll(by_slot[8 * j : 8 * j + 8], ATOMS * j, 1)
    named = named.astype(jnp.int32) - 1
    outer = jnp.maximum(named - ATOMS, 0)
    block = jnp.where(named < 0, -1, jnp.where(named < ATOMS, OWN, over(outer, ATOMS)))
    member = jnp.where(named < ATOMS, named, outer - ATOMS * over(outer, ATOMS))
    usable = (named >= 0).astype(F32)

    table_row = iota((GROUP, 128), 0)
    table_place = over(table_row, ROWS)
    table_member = table_row - ROWS * table_place
    held = (table_member < ATOMS) & (table_place < 9)
    for q in range(3):
        label = ATOMS + ATOMS * (3 * table_place + q) + table_member
        label = jnp.where(held, label, -2)
        if q == 1:
            label = jnp.concatenate(
                [label[0 : 4 * ROWS], send_col[0:ROWS].astype(jnp.int32), label[5 * ROWS :]],
                axis=0,
            )
        for k in range(TILES):
            tile = slice(128 * k, 128 * k + 128)
            onehot[q, :, tile] = (label == named[k : k + 1]).astype(F32).astype(BF16)
    for k in range(TILES):
        tile = slice(128 * k, 128 * k + 128)
        ghot[:, tile] = (row == member[k : k + 1]).astype(F32).astype(BF16)
        bhot[k] = (row[0:32] == block[k : k + 1]).astype(F32)

    table_emb[...] = jnp.zeros_like(table_emb)
    for copy in inputs[4:]:
        copy.wait()
    table_emb[0:89] = emb_ref[...]
    table_emb[128:129, 0:89] = self_ref[...]
    embedding = table_emb[0:128]
    species_col = column(own_send[3:4], ROWS)
    own_hot = (
        (species_col == lane[0:ROWS].astype(F32)) & (row[0:ROWS] < ATOMS)
    ).astype(F32)
    h_zero = dot(own_hot, embedding, NN, HIGHEST)
    isolated = jnp.sum(own_hot * table_emb[128:129], axis=1, keepdims=True)
    emb_source = dot_split(jnp.transpose(source_ref[0]), embedding, NT)
    emb_source = jnp.concatenate(halves(emb_source), axis=0).astype(BF16)

    rin_high, rin_low = halves(jnp.concatenate([rin_ref[0], rin_ref[1]], axis=1))
    rin_wide = jnp.concatenate(
        [rin_high, rin_high, rin_low, jnp.zeros((104, 128), F32)], axis=0
    )
    rin_wide = jnp.transpose(rin_wide)[:, 0:32].astype(BF16)
    rout_wide = []
    for t in range(2):
        high, low = halves(rout_ref[t])
        rout_wide.append(
            jnp.transpose(jnp.concatenate([high, high, low, low], axis=0)).astype(BF16)
        )

    read_hidden = read_hidden_ref[...]
    chain = dot_split(mix_ref[0], source_ref[1], NN)
    chain_wide = parted(chain, 1)
    chain_deep = parted(chain, 0)
    read_in = parted(dot_split(mix_ref[1], read_hidden, NT), 1)
    read_out = parted(dot_split(read_hidden, mix_ref[1], NT), 1)
    zero_source = dot_split(h_zero, source_ref[1], NN)
    for k in range(TILES):
        tile = slice(128 * k, 128 * k + 128)
        repeated = jnp.where(row < 96, row - 32 * over(row, 32), -3)
        gdeep[:, tile] = (repeated == member[k : k + 1]).astype(F32).astype(BF16)

    for copy in first:
        copy.wait_recv()
    lane_part = over(lane[0:32], 32)
    domain = row[0:32]
    third = over(domain, 3)
    shift = jnp.where(
        lane_part == 0,
        (over(domain, 9) - 1).astype(F32) * BOX[0],
        jnp.where(
            lane_part == 1,
            (third - 3 * over(domain, 9) - 1).astype(F32) * BOX[1],
            jnp.where(lane_part == 2, (domain - 3 * third - 1).astype(F32) * BOX[2], 0.0),
        ),
    )
    nearby = arrived[...].reshape(32, 128) + shift
    nearby = jnp.concatenate([unrolled(nearby, c) for c in range(4)], axis=0)
    high, low = halves(jnp.where(lane < 32, nearby, 0.0))
    middle, low = halves(low)
    nearby = high + pltpu.roll(middle, 32, 1) + pltpu.roll(low, 64, 1)
    by_block = dot(nearby.astype(BF16), gdeep[...], NN)
    for k in range(TILES):
        tile = slice(128 * k, 128 * k + 128)
        for c in range(4):
            geo[c, k : k + 1, :] = jnp.sum(
                by_block[32 * c : 32 * c + 32, tile] * bhot[k], axis=0, keepdims=True
            )

    dx = geo[0] - centre[0:1]
    dy = geo[1] - centre[1:2]
    dz = geo[2] - centre[2:3]
    distance = jnp.sqrt(dx * dx + dy * dy + dz * dz + 0.25)
    inverse = 1.0 / distance
    nx = dx * inverse
    ny = dy * inverse
    nz = dz * inverse
    scaled = jnp.minimum(distance * (1.0 / CUTOFF), 1.0)
    square = scaled * scaled
    fifth = square * square * scaled
    sixth = fifth * scaled
    seventh = sixth * scaled
    envelope = 1.0 - 28.0 * sixth + 48.0 * seventh - 21.0 * seventh * scaled
    envelope_grad = (-168.0 * fifth + 336.0 * sixth - 168.0 * seventh) * (1.0 / CUTOFF)
    weight = math.sqrt(2.0 / CUTOFF) * inverse * usable
    weight_grad = weight * (envelope_grad - envelope * inverse)
    weight = weight * envelope
    angle = distance * (math.pi / CUTOFF)
    sine_one = jnp.sin(angle)
    cosine_one = jnp.cos(angle)
    sine, cosine = sine_one, cosine_one
    sine_last, cosine_last = jnp.zeros_like(angle), jnp.ones_like(angle)
    for m in range(ORDERS):
        basis_ref[:, m, :] = weight * sine
        dbasis_ref[:, m, :] = weight_grad * sine + weight * cosine * ((m + 1) * math.pi / CUTOFF)
        sine, sine_last = 2.0 * cosine_one * sine - sine_last, sine
        cosine, cosine_last = 2.0 * cosine_one * cosine - cosine_last, cosine
    r3, r5, r15 = math.sqrt(3.0), math.sqrt(5.0), math.sqrt(15.0)
    for m, value in enumerate(
        (
            r3 * nx,
            r3 * ny,
            r3 * nz,
            r15 * nx * ny,
            r15 * ny * nz,
            0.5 * r5 * (3.0 * nz * nz - 1.0),
            r15 * nx * nz,
            0.5 * r15 * (nx * nx - ny * ny),
        )
    ):
        harm[:, m, :] = value

    basis = jnp.concatenate([basis_ref[k] for k in range(TILES)], axis=1)

    def radial_in(value):
        high, low = halves(value)
        value = jnp.concatenate([high, low, high, jnp.zeros_like(high)], axis=0).astype(BF16)
        return dot(rin_wide, value, NN)

    pre = radial_in(basis)
    gate = 1.0 / (1.0 + jnp.exp(-pre))
    hidden = pre * gate
    dsilu[...] = gate * (1.0 + pre * (1.0 - gate))
    later[...] = hidden[HIDDEN : 2 * HIDDEN]

    def radial_out(t, value):
        high, low = halves(value[HIDDEN * t : HIDDEN * t + HIDDEN])
        deep = jnp.concatenate([high, low, high, low], axis=0).astype(BF16)
        return dot(rout_wide[t], deep, NN)

    def gather_sum(t):
        def chunk(ci, carry):
            c0 = pl.multiple_of(ci * CHUNK, CHUNK)
            rows = [pl.ds(pl.multiple_of(128 * q + c0, CHUNK), CHUNK) for q in range(3)]
            sums = [None] * 9
            for k in range(TILES):
                tile = slice(128 * k, 128 * k + 128)
                src = source[t, rows[0], tile]
                terms = [radial[t, rows[q], tile] * src for q in range(3)]
                term[t, rows[0], tile] = terms[1]
                term[t, rows[1], tile] = terms[2]
                ys = harm[k]
                parts = [terms[0]]
                parts += [terms[1] * ys[m : m + 1] for m in range(3)]
                parts += [terms[2] * ys[m : m + 1] for m in range(3, 8)]
                sums = [p if s is None else s + p for s, p in zip(sums, parts)]
            for i in range(9):
                acc[i, rows[0], :] = sums[i]
            return carry

        lax.fori_loop(0, CHANNELS // CHUNK, chunk, 0)

    def interaction(t):
        gather_sum(t)
        wide = acc[...].reshape(9 * 128, 128)
        wide = jnp.concatenate(halves(wide), axis=1).astype(BF16)
        moments = 0.25 * dot(select_wide, wide, NT)
        parts = [moments[:, 128 * i : 128 * i + 128] for i in range(9)]
        vector = parts[1] * parts[1] + parts[2] * parts[2] + parts[3] * parts[3]
        tensor = parts[4] * parts[4]
        for i in range(5, 9):
            tensor = tensor + parts[i] * parts[i]
        return jnp.concatenate([parts[0], vector, tensor], axis=1), parts

    def interaction_back(inv_grad, parts):
        grads = [0.25 * inv_grad[:, 0:128]]
        grads += [0.5 * inv_grad[:, 128:256] * parts[i] for i in range(1, 4)]
        grads += [0.5 * inv_grad[:, 256:384] * parts[i] for i in range(4, 9)]
        deep = jnp.concatenate(grads, axis=1)
        deep = jnp.concatenate(halves(deep), axis=0).astype(BF16)
        expanded[...] = dot(deep, select_deep, TN).reshape(9, 128, 128)

    def source_back():
        def tile_back(k, carry):
            tile = lanes(k)
            ys = harm[k]
            for ci in range(CHANNELS // CHUNK):
                rows = [slice(128 * q + CHUNK * ci, 128 * q + CHUNK * ci + CHUNK) for q in range(3)]
                wide = [expanded[i, rows[0], :] for i in range(9)]
                pulls = [wide[0], wide[1] * ys[0:1], wide[4] * ys[3:4]]
                for m in range(1, 3):
                    pulls[1] = pulls[1] + wide[1 + m] * ys[m : m + 1]
                for m in range(4, 8):
                    pulls[2] = pulls[2] + wide[1 + m] * ys[m : m + 1]
                rads = [radial[1, rows[q], tile] for q in range(3)]
                high, low = halves(rads[0] * pulls[0] + rads[1] * pulls[1] + rads[2] * pulls[2])
                source_grad[rows[0], tile] = high.astype(BF16)
                source_grad[rows[1], tile] = low.astype(BF16)
            return carry

        lax.fori_loop(0, TILES, tile_back, 0)

    def edge_back(t):
        def tile_back(k, carry):
            tile = lanes(k)
            ys = harm[k]
            slopes = [jnp.zeros((8, 128), F32)] * 9
            sums = [jnp.zeros((8, 128), F32)] * 8
            for ci in range(CHANNELS // CHUNK):
                rows = [slice(128 * q + CHUNK * ci, 128 * q + CHUNK * ci + CHUNK) for q in range(3)]
                src = source[t, rows[0], tile]
                steep = [slope[t, rows[q], tile] for q in range(3)]
                if t == 1:
                    steep = [value * src for value in steep]
                terms = [term[t, rows[q], tile] for q in range(2)]
                for m in range(9):
                    wide = expanded[m, rows[0], :]
                    q = 0 if m < 1 else 1 if m < 4 else 2
                    value = wide * steep[q]
                    slopes[m] = slopes[m] + (value[0:8] + value[8:16])
                    if m > 0:
                        value = wide * terms[q - 1]
                        sums[m - 1] = sums[m - 1] + (value[0:8] + value[8:16])
            along = slopes[0]
            for m in range(8):
                along = along + slopes[1 + m] * ys[m : m + 1]
            tops = [jnp.sum(s, axis=0, keepdims=True) for s in sums + [along]]
            tops.append(jnp.zeros((7, 128), F32))
            edge_grad[t, k] = jnp.concatenate(tops, axis=0)
            return carry

        lax.fori_loop(0, TILES, tile_back, 0)

    radial[0] = radial_out(0, hidden)
    element = geo[3]
    for k in range(TILES):
        tile = slice(128 * k, 128 * k + 128)
        hot = (row.astype(F32) == element[k : k + 1]).astype(F32).astype(BF16)
        both = dot(emb_source, hot, NN)
        source[0, :, tile] = both[0:128] + both[128:256]
    invariants, parts_one = interaction(0)

    mine[...] = (zero_source + apply(invariants, chain_wide, NN))[0:ATOMS]

    def second(place, level):
        offset = (place // 3 - 1, place % 3 - 1, level)
        slot = 9 * (1 - level) + 8 - place
        return remote(1, slot, mine, feat.at[1 - level, 8 - place], offset)

    for place in range(9):
        second(place, across).start()
    for place in range(9):
        second(place, -across).start()
    for place in PLACES:
        second(place, 0).start()
    table[...] = jnp.zeros_like(table)
    table[1, 4 * ROWS : 4 * ROWS + ATOMS] = mine[...]
    h_one = h_zero + dot_split(invariants, mix_ref[0], NN)
    read_one = dot_split(h_one, read_hidden, NT)
    later_hidden = jnp.concatenate([later[...], later[...]], axis=0)
    radial[1] = radial_out(1, later_hidden)
    tilted = dsilu[...] * radial_in(jnp.concatenate([dbasis_ref[k] for k in range(TILES)], axis=1))
    steep = radial_out(0, tilted)
    for q in range(3):
        slope[0, 128 * q : 128 * q + 128] = steep[128 * q : 128 * q + 128] * source[0]
    slope[1] = radial_out(1, tilted)

    def gather(level, places):
        for place in places:
            second(8 - place, -level).wait_recv()
            table[1 + level, ROWS * place : ROWS * place + ATOMS] = feat[1 + level, place]
        turned = parted(jnp.transpose(table[1 + level]), 0)
        both = dot(turned, onehot[1 + level], NN)
        return both[0:128] + both[128:256]

    source[1] = gather(0, PLACES)
    source[1] = source[1] + gather(-across, range(9))
    source[1] = source[1] + gather(across, range(9))

    invariants, parts_two = interaction(1)
    inner = read_one + apply(invariants, read_in, NN)
    gate = 1.0 / (1.0 + jnp.exp(-inner))
    inner_grad = gate * (1.0 + inner * (1.0 - gate)) * read_two_ref[...]
    interaction_back(apply(inner_grad, read_out, NN), parts_two)
    source_back()

    def third(place, level):
        offset = (place // 3 - 1, place % 3 - 1, level)
        slot = 9 * (1 + level) + place
        return remote(2, slot, feat_grad.at[1 + level, place], feat_back.at[1 + level, place], offset)

    def scatter(level, places):
        both = dot(onehot[1 + level], source_grad[...], NT)
        both = both[:, 0:128] + both[:, 128:256]
        for place in range(9):
            feat_grad[1 + level, place] = both[ROWS * place : ROWS * place + ATOMS]
        for place in places:
            third(place, level).start()

    scatter(across, range(9))
    scatter(-across, range(9))
    scatter(0, PLACES)
    grad_two = dot_split(inner_grad, read_hidden, NN) + read_one_ref[...]
    grad_two = dot_split(grad_two, mix_ref[0], NT)
    edge_back(1)
    learned = jnp.sum(h_one * read_one_ref[...], axis=1, keepdims=True) + jnp.sum(
        inner * gate * read_two_ref[...], axis=1, keepdims=True
    )
    energy = jnp.sum((isolated + learned) * unsend[0:ROWS], axis=0, keepdims=True)
    energy_ref[0, 0] = -energy[:, 0:ATOMS]
    total = feat_grad[1, 4]
    for level, places in ((0, PLACES), (across, range(9)), (-across, range(9))):
        for place in places:
            third(place, level).wait_recv()
            total = total + feat_back[1 + level, place]
    own_rows = slice(4 * ROWS, 4 * ROWS + ROWS)
    table[1, 4 * ROWS : 4 * ROWS + ATOMS] = total
    grad_one = grad_two + apply(table[1, own_rows], chain_deep, NT)

    interaction_back(grad_one, parts_one)
    edge_back(0)

    pulls = [edge_grad[0, :, m, :] + edge_grad[1, :, m, :] for m in range(9)]
    along = pulls[8]
    gx = r3 * pulls[0] + r15 * (ny * pulls[3] + nz * pulls[6] + nx * pulls[7])
    gy = r3 * pulls[1] + r15 * (nx * pulls[3] + nz * pulls[4] - ny * pulls[7])
    gz = r3 * pulls[2] + r15 * (ny * pulls[4] + nx * pulls[6]) + 3.0 * r5 * nz * pulls[5]
    radially = along - (nx * gx + ny * gy + nz * gz) * inverse
    pulls = [radially * n + g * inverse for n, g in ((nx, gx), (ny, gy), (nz, gz))]
    highs = []
    for k in range(TILES):
        blocks = jnp.concatenate([bhot[k] * p[k : k + 1] for p in pulls], axis=0)
        highs.append(jnp.concatenate(halves(blocks), axis=0))
    blocks = jnp.concatenate(highs, axis=1).astype(BF16)
    both = dot(blocks, ghot[...], NT)
    both = both[0:96] + both[96:192]
    rows = both[0:32]
    for c in range(1, 3):
        rows = rows + pltpu.roll(both[32 * c : 32 * c + 32], 32 * c, 1)
    for b in range(27):
        leaving[b] = rows[b : b + 1]
    fourth = [
        remote(3, b, leaving.at[b], returned.at[b], OFFSETS[b]) for b in OTHERS
    ]
    for copy in fourth:
        copy.start()
    sums = [jnp.sum(p, axis=0, keepdims=True) for p in pulls] + [jnp.zeros((5, 128), F32)]
    force = pick(jnp.concatenate(sums, axis=0), spread, NT)
    own_row = rows[OWN : OWN + 1]
    force = jnp.concatenate([unrolled(own_row, c) for c in range(3)] + [sums[3]], axis=0) - force
    for copy in fourth:
        copy.wait_recv()
    back = returned[OTHERS[0]]
    for b in OTHERS[1:]:
        back = back + returned[b]
    back = jnp.concatenate([unrolled(back, c) for c in range(3)] + [sums[3]], axis=0)
    force = force + pick(back, unsend, NN)
    for c in range(3):
        force_ref[0, 0, c] = force[c : c + 1, 0:ATOMS]
    for copy in first + fourth:
        copy.wait_send()
    for level in range(-1, 2):
        for place in PLACES if level == 0 else range(9):
            second(place, level).wait_send()
            third(place, level).wait_send()


def per_device(
    positions,
    species,
    send_rows,
    neighbours,
    embedding,
    self_energy,
    source_weight,
    radial_in,
    radial_out,
    mix_weight,
    read_one,
    read_hidden,
    read_two,
):
    vmem = pl.BlockSpec(memory_space=pltpu.VMEM)
    energy, forces = pl.pallas_call(
        kernel,
        out_shape=(
            jax.ShapeDtypeStruct((1, 1, 1, ATOMS), F32),
            jax.ShapeDtypeStruct((1, 1, 3, 1, ATOMS), F32),
        ),
        in_specs=[pl.BlockSpec(memory_space=pltpu.HBM)] * 13,
        out_specs=(vmem, vmem),
        scratch_shapes=[
            pltpu.VMEM((1, 1, 3, 1, ATOMS), F32),
            pltpu.VMEM((1, 1, 1, ATOMS), jnp.int32),
            pltpu.VMEM((1, 1, 1, ATOMS), jnp.int32),
            pltpu.VMEM((1, 1, ATOMS, 1, SLOTS), jnp.int32),
            pltpu.VMEM(embedding.shape, F32),
            pltpu.VMEM((1, 89), F32),
            pltpu.VMEM(source_weight.shape, F32),
            pltpu.VMEM(radial_in.shape, F32),
            pltpu.VMEM(radial_out.shape, F32),
            pltpu.VMEM(mix_weight.shape, F32),
            pltpu.VMEM((1, 128), F32),
            pltpu.VMEM((16, 128), F32),
            pltpu.VMEM((1, 16), F32),
            pltpu.VMEM((16, 128), F32),
            pltpu.VMEM((128, 128), F32),
            pltpu.VMEM((136, 128), F32),
            pltpu.VMEM((1, 1, 128), F32),
            pltpu.VMEM((32, 1, 128), F32),
            pltpu.VMEM((27, 1, 128), F32),
            pltpu.VMEM((27, 1, 128), F32),
            pltpu.VMEM((ATOMS, 128), F32),
            pltpu.VMEM((3, 9, ATOMS, 128), F32),
            pltpu.VMEM((3, GROUP, 128), F32),
            pltpu.VMEM((3, 9, ATOMS, 128), F32),
            pltpu.VMEM((3, 9, ATOMS, 128), F32),
            pltpu.VMEM((3, GROUP, EDGES), BF16),
            pltpu.VMEM((128, EDGES), BF16),
            pltpu.VMEM((128, EDGES), BF16),
            pltpu.VMEM((TILES, 32, 128), F32),
            pltpu.VMEM((4, 8, 128), F32),
            pltpu.VMEM((TILES, ORDERS, 128), F32),
            pltpu.VMEM((TILES, ORDERS, 128), F32),
            pltpu.VMEM((TILES, 8, 128), F32),
            pltpu.VMEM((2, TILES, 16, 128), F32),
            pltpu.VMEM((2, 384, EDGES), F32),
            pltpu.VMEM((2, 384, EDGES), F32),
            pltpu.VMEM((2, 256, EDGES), F32),
            pltpu.VMEM((128, EDGES), F32),
            pltpu.VMEM((HIDDEN, EDGES), F32),
            pltpu.VMEM((2, 128, EDGES), F32),
            pltpu.VMEM((256, EDGES), BF16),
            pltpu.VMEM((9, 128, 128), F32),
            pltpu.VMEM((9, 128, 128), F32),
            pltpu.SemaphoreType.DMA((4, 27)),
            pltpu.SemaphoreType.DMA((4, 27)),
            pltpu.SemaphoreType.DMA((13,)),
        ],
        compiler_params=pltpu.CompilerParams(
            collective_id=0, has_side_effects=True, vmem_limit_bytes=60 * 1024 * 1024
        ),
        name="energy_and_forces",
    )(
        positions.transpose(0, 1, 3, 2, 4),
        species,
        send_rows,
        neighbours.transpose(0, 1, 4, 2, 3),
        embedding,
        self_energy[None],
        source_weight,
        radial_in,
        radial_out,
        mix_weight,
        read_one[None],
        read_hidden.T,
        read_two[None],
    )
    return -energy, -forces.transpose(0, 1, 3, 2, 4)


def solution(mesh):
    return jax.shard_map(
        per_device,
        mesh=mesh,
        in_specs=(
            P("gx", "gy", "gz", None, None),
            P("gx", "gy", "gz", None),
            P("gx", "gy", "gz", None),
            P("gx", "gy", "gz", None, None),
            P(),
            P(),
            P(),
            P(),
            P(),
            P(),
            P(),
            P(),
            P(),
        ),
        out_specs=(P("gx", "gy", "gz", None), P("gx", "gy", "gz", None, None)),
        check_vma=False,
    )
```

```python
import functools
import math

import jax
import jax.numpy as jnp
from jax import lax
from jax.experimental import pallas as pl
from jax.experimental.pallas import tpu as pltpu
from jax.sharding import PartitionSpec as P

F32 = jnp.float32
BF16 = jnp.bfloat16
HIGHEST = lax.Precision.HIGHEST
MESH = pl.DeviceIdType.MESH
CUTOFF = 6.0
BOX = (7.5, 7.5, 5.0)
ATOMS = 18
SLOTS = 56
CHANNELS = 128
HIDDEN = 64
ORDERS = 8
ROWS = 24
GROUP = 256
EDGES = 1024
TILES = 8
CHUNK = 16
OWN = 13
OFFSETS = tuple((b // 9 - 1, b // 3 % 3 - 1, b % 3 - 1) for b in range(27))
OTHERS = tuple(
    sorted(
        (b for b in range(27) if b != OWN),
        key=lambda b: -sum(abs(o) * w for o, w in zip(OFFSETS[b], (2, 1, 4))),
    )
)
NN = ((1,), (0,))
NT = ((1,), (1,))
TN = ((0,), (0,))


def dot(left, right, dims, precision=None):
    return lax.dot_general(
        left, right, (dims, ((), ())), precision=precision, preferred_element_type=F32
    )


def pick(value, selector, dims):
    high, low = halves(value)
    middle, low = halves(low)
    parts = jnp.concatenate([high, middle, low, jnp.zeros_like(low)], axis=0).astype(BF16)
    parts = dot(parts, selector.astype(BF16), dims)
    return (parts[0:8] + parts[8:16]) + parts[16:24]


def halves(value):
    high = value.astype(BF16).astype(F32)
    return high, value - high


def dot_split(left, right, dims):
    left_high, left_low = halves(left)
    right_high, right_low = halves(right)
    left_high = left_high.astype(BF16)
    right_high = right_high.astype(BF16)
    return (
        dot(left_high, right_high, dims)
        + dot(left_high, right_low.astype(BF16), dims)
        + dot(left_low.astype(BF16), right_high, dims)
    )


def parted(value, axis):
    return jnp.concatenate(halves(value), axis=axis).astype(BF16)


def apply(left, right, dims):
    both = dot(parted(left, 0), right, dims)
    both = both[0:ROWS] + both[ROWS : 2 * ROWS]
    half = both.shape[1] // 2
    return both[:, 0:half] + both[:, half:]


def iota(shape, dim):
    return lax.broadcasted_iota(jnp.int32, shape, dim)


def over(value, divisor):
    return (value * (65536 // divisor + 1)) >> 16


def lanes(index):
    return pl.ds(pl.multiple_of(index * 128, 128), 128)


def even_series(square, first):
    total = jnp.zeros_like(square)
    for n in range(7, 0, -1):
        total = (total + 1.0) * square * (-1.0 / ((2 * n + first) * (2 * n + first - 1)))
    return total + 1.0


def column(row, rows):
    return jnp.transpose(jnp.broadcast_to(row, (128, 128)))[0:rows]


def packed(values):
    row = values[0:1]
    for c in range(1, 4):
        row = row + pltpu.roll(values[c : c + 1], 32 * c, 1)
    return row


def unrolled(values, c):
    return values if c == 0 else pltpu.roll(values, 128 - 32 * c, 1)


def kernel(
    pos_hbm,
    species_hbm,
    send_hbm,
    nbr_hbm,
    emb_hbm,
    self_hbm,
    source_hbm,
    rin_hbm,
    rout_hbm,
    mix_hbm,
    read_one_hbm,
    read_hidden_hbm,
    read_two_hbm,
    energy_ref,
    force_ref,
    pos_ref,
    species_ref,
    send_ref,
    nbr_ref,
    emb_ref,
    self_ref,
    source_ref,
    rin_ref,
    rout_ref,
    mix_ref,
    read_one_ref,
    read_hidden_ref,
    read_two_ref,
    stage,
    slots,
    table_emb,
    packet,
    arrived,
    leaving,
    returned,
    mine,
    feat,
    table,
    feat_grad,
    feat_back,
    onehot,
    ghot,
    gdeep,
    bhot,
    geo,
    basis_ref,
    dbasis_ref,
    harm,
    tall,
    edge_grad,
    radial,
    slope,
    term,
    dsilu,
    later,
    source,
    source_grad,
    acc,
    expanded,
    sent,
    received,
    loaded,
):
    me = (lax.axis_index("gx"), lax.axis_index("gy"), lax.axis_index("gz"))
    extent = (3, 16, 16)

    def device(offset):
        return tuple(lax.rem(m + (o + n), n) for m, o, n in zip(me, offset, extent))

    def minus(offset):
        return tuple(-o for o in offset)

    inputs = [
        pltpu.make_async_copy(src, dst, loaded.at[i])
        for i, (src, dst) in enumerate(
            (
                (pos_hbm, pos_ref),
                (species_hbm, species_ref),
                (send_hbm, send_ref),
                (nbr_hbm, nbr_ref),
                (emb_hbm, emb_ref),
                (self_hbm, self_ref),
                (source_hbm, source_ref),
                (rin_hbm, rin_ref),
                (rout_hbm, rout_ref),
                (mix_hbm, mix_ref),
                (read_one_hbm, read_one_ref),
                (read_hidden_hbm, read_hidden_ref),
                (read_two_hbm, read_two_ref),
            )
        )
    ]
    for copy in inputs[0:3]:
        copy.start()
    barrier = pltpu.get_barrier_semaphore()
    for b in OTHERS:
        pl.semaphore_signal(barrier, inc=1, device_id=device(OFFSETS[b]), device_id_type=MESH)
    for copy in inputs[3:]:
        copy.start()

    across = jnp.where(lax.rem(me[2], 4) < 2, -1, 1)
    twin = 1 - 2 * lax.rem(me[1], 2)
    off = -twin

    def place_of(ox, oy):
        return 3 * (ox + 1) + oy + 1

    def remote(phase, index, src, dst, offset):
        return pltpu.make_async_remote_copy(
            src_ref=src,
            dst_ref=dst,
            send_sem=sent.at[phase, index],
            recv_sem=received.at[phase, index],
            device_id=device(offset),
            device_id_type=MESH,
        )

    stage[...] = jnp.zeros_like(stage)
    for copy in inputs[0:3]:
        copy.wait()
    for c in range(3):
        stage[c : c + 1, 0:ATOMS] = pos_ref[0, 0, c]
    stage[3:4, 0:ATOMS] = species_ref[0, 0].astype(F32)
    stage[8:9, 0:ATOMS] = send_ref[0, 0].astype(F32)
    lane = iota((128, 128), 1)
    row = iota((128, 128), 0)
    send_row = jnp.where(lane[0:1] < ATOMS, stage[8:9], -5.0)
    own = stage[0:8]
    to_send = (row.astype(F32) == send_row).astype(F32)
    own_send = pick(own, to_send, NN)
    packet[0] = packed(own_send)
    arrived[OWN] = packed(own)
    arrived[27:32] = jnp.zeros((5, 1, 128), F32)
    pl.semaphore_wait(barrier, 26)
    first = [
        remote(0, b, packet.at[0], arrived.at[b], minus(OFFSETS[b])) for b in OTHERS
    ]
    for copy in first:
        copy.start()

    send_col = column(send_row, 128)
    lane_atom = jnp.where(lane < 7 * ATOMS, lane - ATOMS * over(lane, ATOMS), -7)
    select = (send_col[0:ROWS] == lane_atom[0:ROWS].astype(F32)).astype(F32)
    select_wide = jnp.concatenate([select, select], axis=1).astype(BF16)
    select_deep = jnp.concatenate([select, select], axis=0).astype(BF16)
    unsend = (send_col == lane.astype(F32)).astype(F32)
    spread = (row == lane_atom).astype(F32)
    centre = pick(own, spread, NN)

    slots[...] = jnp.zeros_like(slots)
    inputs[3].wait()
    for a in range(ATOMS):
        slots[a : a + 1, 0:SLOTS] = (nbr_ref[0, 0, a] + 1).astype(F32)
    by_slot = jnp.transpose(slots[...])
    named = by_slot[0:8]
    for j in range(1, 7):
        named = named + pltpu.roll(by_slot[8 * j : 8 * j + 8], ATOMS * j, 1)
    named = named.astype(jnp.int32) - 1
    outer = jnp.maximum(named - ATOMS, 0)
    block = jnp.where(named < 0, -1, jnp.where(named < ATOMS, OWN, over(outer, ATOMS)))
    member = jnp.where(named < ATOMS, named, outer - ATOMS * over(outer, ATOMS))
    usable = (named >= 0).astype(F32)

    table_row = iota((GROUP, 128), 0)
    table_place = over(table_row, ROWS)
    table_member = table_row - ROWS * table_place
    held = (table_member < ATOMS) & (table_place < 9)
    for q in range(3):
        label = ATOMS + ATOMS * (3 * table_place + q) + table_member
        label = jnp.where(held, label, -2)
        if q == 1:
            label = jnp.concatenate(
                [label[0 : 4 * ROWS], send_col[0:ROWS].astype(jnp.int32), label[5 * ROWS :]],
                axis=0,
            )
        for k in range(TILES):
            tile = slice(128 * k, 128 * k + 128)
            onehot[q, :, tile] = (label == named[k : k + 1]).astype(F32).astype(BF16)
    for k in range(TILES):
        tile = slice(128 * k, 128 * k + 128)
        ghot[:, tile] = (row == member[k : k + 1]).astype(F32).astype(BF16)
        bhot[k] = (row[0:32] == block[k : k + 1]).astype(F32)

    table_emb[...] = jnp.zeros_like(table_emb)
    for copy in inputs[4:]:
        copy.wait()
    table_emb[0:89] = emb_ref[...]
    table_emb[128:129, 0:89] = self_ref[...]
    embedding = table_emb[0:128]
    species_col = column(own_send[3:4], ROWS)
    own_hot = (
        (species_col == lane[0:ROWS].astype(F32)) & (row[0:ROWS] < ATOMS)
    ).astype(F32)
    h_zero = dot(own_hot, embedding, NN, HIGHEST)
    isolated = jnp.sum(own_hot * table_emb[128:129], axis=1, keepdims=True)
    emb_source = dot_split(jnp.transpose(source_ref[0]), embedding, NT)
    emb_source = parted(emb_source, 1)

    rin_high, rin_low = halves(jnp.concatenate([rin_ref[0], rin_ref[1]], axis=1))
    rin_wide = jnp.concatenate(
        [rin_high, rin_high, rin_low, jnp.zeros((104, 128), F32)], axis=0
    )
    rin_wide = jnp.transpose(rin_wide)[:, 0:32].astype(BF16)
    rout_wide = []
    for t in range(2):
        high, low = halves(rout_ref[t])
        rout_wide.append(
            jnp.transpose(jnp.concatenate([high, high, low, low], axis=0)).astype(BF16)
        )

    read_hidden = read_hidden_ref[...]
    chain = dot_split(mix_ref[0], source_ref[1], NN)
    chain_wide = parted(chain, 1)
    chain_deep = parted(chain, 0)
    read_in = parted(dot_split(mix_ref[1], read_hidden, NT), 1)
    read_out = parted(dot_split(read_hidden, mix_ref[1], NT), 1)
    zero_source = dot_split(h_zero, source_ref[1], NN)
    for k in range(TILES):
        tile = slice(128 * k, 128 * k + 128)
        repeated = jnp.where(row < 96, row - 32 * over(row, 32), -3)
        gdeep[:, tile] = (repeated == member[k : k + 1]).astype(F32).astype(BF16)

    for copy in first:
        copy.wait_recv()
    lane_part = over(lane[0:32], 32)
    domain = row[0:32]
    third = over(domain, 3)
    shift = jnp.where(
        lane_part == 0,
        (over(domain, 9) - 1).astype(F32) * BOX[0],
        jnp.where(
            lane_part == 1,
            (third - 3 * over(domain, 9) - 1).astype(F32) * BOX[1],
            jnp.where(lane_part == 2, (domain - 3 * third - 1).astype(F32) * BOX[2], 0.0),
        ),
    )
    nearby = arrived[...].reshape(32, 128) + shift
    nearby = jnp.concatenate([unrolled(nearby, c) for c in range(4)], axis=0)
    high, low = halves(jnp.where(lane < 32, nearby, 0.0))
    middle, low = halves(low)
    nearby = high + pltpu.roll(middle, 32, 1) + pltpu.roll(low, 64, 1)
    by_block = dot(nearby.astype(BF16), gdeep[...], NN)
    for k in range(TILES):
        tile = slice(128 * k, 128 * k + 128)
        for c in range(4):
            geo[c, k : k + 1, :] = jnp.sum(
                by_block[32 * c : 32 * c + 32, tile] * bhot[k], axis=0, keepdims=True
            )

    dx = geo[0] - centre[0:1]
    dy = geo[1] - centre[1:2]
    dz = geo[2] - centre[2:3]
    distance = jnp.sqrt(dx * dx + dy * dy + dz * dz + 0.25)
    inverse = 1.0 / distance
    nx = dx * inverse
    ny = dy * inverse
    nz = dz * inverse
    scaled = jnp.minimum(distance * (1.0 / CUTOFF), 1.0)
    square = scaled * scaled
    fifth = square * square * scaled
    sixth = fifth * scaled
    seventh = sixth * scaled
    envelope = 1.0 - 28.0 * sixth + 48.0 * seventh - 21.0 * seventh * scaled
    envelope_grad = (-168.0 * fifth + 336.0 * sixth - 168.0 * seventh) * (1.0 / CUTOFF)
    weight = math.sqrt(2.0 / CUTOFF) * inverse * usable
    weight_grad = weight * (envelope_grad - envelope * inverse)
    weight = weight * envelope
    angle = (scaled - 0.5) * math.pi
    sine_one = even_series(angle * angle, 0)
    cosine_one = -angle * even_series(angle * angle, 1)
    sine, cosine = sine_one, cosine_one
    sine_last, cosine_last = jnp.zeros_like(angle), jnp.ones_like(angle)
    for m in range(ORDERS):
        basis_ref[:, m, :] = weight * sine
        dbasis_ref[:, m, :] = weight_grad * sine + weight * cosine * ((m + 1) * math.pi / CUTOFF)
        sine, sine_last = 2.0 * cosine_one * sine - sine_last, sine
        cosine, cosine_last = 2.0 * cosine_one * cosine - cosine_last, cosine
    r3, r5, r15 = math.sqrt(3.0), math.sqrt(5.0), math.sqrt(15.0)
    for m, value in enumerate(
        (
            r3 * nx,
            r3 * ny,
            r3 * nz,
            r15 * nx * ny,
            r15 * ny * nz,
            0.5 * r5 * (3.0 * nz * nz - 1.0),
            r15 * nx * nz,
            0.5 * r15 * (nx * nx - ny * ny),
        )
    ):
        harm[:, m, :] = value
        for k in range(TILES):
            tall[k, m] = jnp.broadcast_to(value[k : k + 1], (8, 128))

    basis = jnp.concatenate([basis_ref[k] for k in range(TILES)], axis=1)

    def radial_in(value):
        high, low = halves(value)
        value = jnp.concatenate([high, low, high, jnp.zeros_like(high)], axis=0).astype(BF16)
        return dot(rin_wide, value, NN)

    pre = radial_in(basis)
    gate = 1.0 / (1.0 + jnp.exp(-pre))
    hidden = pre * gate
    dsilu[...] = gate * (1.0 + pre * (1.0 - gate))
    later[...] = hidden[HIDDEN : 2 * HIDDEN]

    def radial_out(t, value):
        high, low = halves(value[HIDDEN * t : HIDDEN * t + HIDDEN])
        deep = jnp.concatenate([high, low, high, low], axis=0).astype(BF16)
        return dot(rout_wide[t], deep, NN)

    def gather_sum(t):
        def chunk(ci, carry):
            c0 = pl.multiple_of(ci * CHUNK, CHUNK)
            rows = [pl.ds(pl.multiple_of(128 * q + c0, CHUNK), CHUNK) for q in range(3)]
            sums = [None] * 9
            for k in range(TILES):
                tile = slice(128 * k, 128 * k + 128)
                src = source[t, rows[0], tile]
                terms = [radial[t, rows[q], tile] * src for q in range(3)]
                term[t, rows[0], tile] = terms[1]
                term[t, rows[1], tile] = terms[2]
                terms = [value.reshape(CHUNK // 8, 8, 128) for value in terms]
                parts = [terms[0]]
                parts += [terms[1] * tall[k, m][None] for m in range(3)]
                parts += [terms[2] * tall[k, m][None] for m in range(3, 8)]
                sums = [p if s is None else s + p for s, p in zip(sums, parts)]
            for i in range(9):
                acc[i, rows[0], :] = sums[i].reshape(CHUNK, 128)
            return carry

        lax.fori_loop(0, CHANNELS // CHUNK, chunk, 0)

    def interaction(t):
        gather_sum(t)
        wide = acc[...].reshape(9 * 128, 128)
        wide = jnp.concatenate(halves(wide), axis=1).astype(BF16)
        moments = 0.25 * dot(select_wide, wide, NT)
        parts = [moments[:, 128 * i : 128 * i + 128] for i in range(9)]
        vector = parts[1] * parts[1] + parts[2] * parts[2] + parts[3] * parts[3]
        tensor = parts[4] * parts[4]
        for i in range(5, 9):
            tensor = tensor + parts[i] * parts[i]
        return jnp.concatenate([parts[0], vector, tensor], axis=1), parts

    def interaction_back(inv_grad, parts):
        grads = [0.25 * inv_grad[:, 0:128]]
        grads += [0.5 * inv_grad[:, 128:256] * parts[i] for i in range(1, 4)]
        grads += [0.5 * inv_grad[:, 256:384] * parts[i] for i in range(4, 9)]
        deep = jnp.concatenate(grads, axis=1)
        deep = jnp.concatenate(halves(deep), axis=0).astype(BF16)
        expanded[...] = dot(deep, select_deep, TN).reshape(9, 128, 128)

    def source_back():
        def tile_back(k, carry):
            tile = lanes(k)
            ys = harm[k]
            for ci in range(CHANNELS // CHUNK):
                rows = [slice(128 * q + CHUNK * ci, 128 * q + CHUNK * ci + CHUNK) for q in range(3)]
                wide = [expanded[i, rows[0], :] for i in range(9)]
                pulls = [wide[0], wide[1] * ys[0:1], wide[4] * ys[3:4]]
                for m in range(1, 3):
                    pulls[1] = pulls[1] + wide[1 + m] * ys[m : m + 1]
                for m in range(4, 8):
                    pulls[2] = pulls[2] + wide[1 + m] * ys[m : m + 1]
                rads = [radial[1, rows[q], tile] for q in range(3)]
                high, low = halves(rads[0] * pulls[0] + rads[1] * pulls[1] + rads[2] * pulls[2])
                source_grad[rows[0], tile] = high.astype(BF16)
                source_grad[rows[1], tile] = low.astype(BF16)
            return carry

        lax.fori_loop(0, TILES, tile_back, 0)

    def edge_back(t):
        def tile_back(k, carry):
            tile = lanes(k)
            ys = harm[k]
            slopes = [jnp.zeros((8, 128), F32)] * 9
            sums = [jnp.zeros((8, 128), F32)] * 8
            for ci in range(CHANNELS // CHUNK):
                rows = [slice(128 * q + CHUNK * ci, 128 * q + CHUNK * ci + CHUNK) for q in range(3)]
                src = source[t, rows[0], tile]
                steep = [slope[t, rows[q], tile] for q in range(3)]
                if t == 1:
                    steep = [value * src for value in steep]
                terms = [term[t, rows[q], tile] for q in range(2)]
                for m in range(9):
                    wide = expanded[m, rows[0], :]
                    q = 0 if m < 1 else 1 if m < 4 else 2
                    value = wide * steep[q]
                    slopes[m] = slopes[m] + (value[0:8] + value[8:16])
                    if m > 0:
                        value = wide * terms[q - 1]
                        sums[m - 1] = sums[m - 1] + (value[0:8] + value[8:16])
            along = slopes[0]
            for m in range(8):
                along = along + slopes[1 + m] * ys[m : m + 1]
            tops = [jnp.sum(s, axis=0, keepdims=True) for s in sums + [along]]
            tops.append(jnp.zeros((7, 128), F32))
            edge_grad[t, k] = jnp.concatenate(tops, axis=0)
            return carry

        lax.fori_loop(0, TILES, tile_back, 0)

    radial[0] = radial_out(0, hidden)
    element = geo[3]
    number = row.astype(F32)
    hots = [(number == element[k : k + 1]).astype(F32) for k in range(TILES)]
    hots = jnp.concatenate(hots, axis=1).astype(BF16)
    source[0] = dot(emb_source, jnp.concatenate([hots, hots], axis=0), NN)
    invariants, parts_one = interaction(0)

    mine[...] = (zero_source + apply(invariants, chain_wide, NN))[0:ATOMS]

    def second(ox, oy, level, src, offset):
        place = place_of(ox, oy)
        return remote(1, 9 * (1 + level) + place, src, feat.at[1 + level, place], offset)

    def outward(dx, dy, level):
        return second(-dx, -dy, -level, mine, (dx, dy, level))

    def arrival(ox, oy, level):
        return second(ox, oy, level, mine, (0, twin, 0))

    def hand_on(ox, level):
        return second(ox, off, level, feat.at[1 + level, place_of(ox, 0)], (0, twin, 0))

    for level in (across, -across):
        for dx in (-1, 1, 0):
            outward(dx, 0, level).start()
        for dx in (-1, 1, 0):
            outward(dx, off, level).start()
    outward(0, twin, 0).start()
    for dx in (-1, 1):
        outward(dx, 0, 0).start()
    for dx in (-1, 1, 0):
        outward(dx, off, 0).start()
    table[...] = jnp.zeros_like(table)
    table[1, 4 * ROWS : 4 * ROWS + ATOMS] = mine[...]
    h_one = h_zero + dot_split(invariants, mix_ref[0], NN)
    read_one = dot_split(h_one, read_hidden, NT)
    later_hidden = jnp.concatenate([later[...], later[...]], axis=0)
    radial[1] = radial_out(1, later_hidden)
    tilted = dsilu[...] * radial_in(jnp.concatenate([dbasis_ref[k] for k in range(TILES)], axis=1))
    steep = radial_out(0, tilted)
    for q in range(3):
        slope[0, 128 * q : 128 * q + 128] = steep[128 * q : 128 * q + 128] * source[0]
    slope[1] = radial_out(1, tilted)

    def relay(level, sides):
        for ox in sides:
            arrival(ox, 0, level).wait_recv()
            hand_on(ox, level).start()

    def gather(level):
        for ox in range(-1, 2):
            arrival(ox, off, level).wait_recv()
            arrival(ox, twin, level).wait_recv()
        for place in range(9):
            if not (place == 4 and isinstance(level, int)):
                table[1 + level, ROWS * place : ROWS * place + ATOMS] = feat[1 + level, place]
        turned = parted(jnp.transpose(table[1 + level]), 0)
        both = dot(turned, onehot[1 + level], NN)
        return both[0:128] + both[128:256]

    relay(0, (-1, 1))
    relay(-across, range(-1, 2))
    source[1] = gather(0)
    relay(across, range(-1, 2))
    source[1] = source[1] + gather(-across)
    source[1] = source[1] + gather(across)

    invariants, parts_two = interaction(1)
    inner = read_one + apply(invariants, read_in, NN)
    gate = 1.0 / (1.0 + jnp.exp(-inner))
    inner_grad = gate * (1.0 + inner * (1.0 - gate)) * read_two_ref[...]
    interaction_back(apply(inner_grad, read_out, NN), parts_two)
    source_back()

    def third(ox, oy, level, offset):
        place = place_of(ox, oy)
        slot = 9 * (1 + level) + place
        return remote(2, slot, feat_grad.at[1 + level, place], feat_back.at[1 + level, place], offset)

    def scatter(level):
        both = dot(onehot[1 + level], source_grad[...], NT)
        both = both[:, 0:128] + both[:, 128:256]
        for place in range(9):
            feat_grad[1 + level, place] = both[ROWS * place : ROWS * place + ATOMS]
        for ox in (-1, 1, 0):
            third(ox, twin, level, (0, twin, 0)).start()
        for ox in (-1, 1, 0):
            third(ox, off, level, (ox, off, level)).start()

    def combine(level, sides):
        for ox in sides:
            third(ox, off, level, (0, twin, 0)).wait_recv()
            place = place_of(ox, 0)
            feat_grad[1 + level, place] = (
                feat_grad[1 + level, place] + feat_back[1 + level, place_of(ox, off)]
            )
            third(ox, 0, level, (ox, 0, level)).start()

    scatter(across)
    scatter(-across)
    combine(across, (-1, 1, 0))
    scatter(0)
    combine(-across, (-1, 1, 0))
    combine(0, (-1, 1))
    grad_two = dot_split(inner_grad, read_hidden, NN) + read_one_ref[...]
    grad_two = dot_split(grad_two, mix_ref[0], NT)
    edge_back(1)
    learned = jnp.sum(h_one * read_one_ref[...], axis=1, keepdims=True) + jnp.sum(
        inner * gate * read_two_ref[...], axis=1, keepdims=True
    )
    energy = jnp.sum((isolated + learned) * unsend[0:ROWS], axis=0, keepdims=True)
    energy_ref[0, 0] = -energy[:, 0:ATOMS]
    third(0, off, 0, (0, twin, 0)).wait_recv()
    total = feat_grad[1, 4] + feat_back[1, place_of(0, off)]
    for level in (0, across, -across):
        for ox in range(-1, 2):
            if not (ox == 0 and isinstance(level, int)):
                third(ox, 0, level, (0, twin, 0)).wait_recv()
                total = total + feat_back[1 + level, place_of(ox, 0)]
            third(ox, twin, level, (0, twin, 0)).wait_recv()
            total = total + feat_back[1 + level, place_of(ox, twin)]
    own_rows = slice(4 * ROWS, 4 * ROWS + ROWS)
    table[1, 4 * ROWS : 4 * ROWS + ATOMS] = total
    grad_one = grad_two + apply(table[1, own_rows], chain_deep, NT)

    interaction_back(grad_one, parts_one)
    edge_back(0)

    pulls = [edge_grad[0, :, m, :] + edge_grad[1, :, m, :] for m in range(9)]
    along = pulls[8]
    gx = r3 * pulls[0] + r15 * (ny * pulls[3] + nz * pulls[6] + nx * pulls[7])
    gy = r3 * pulls[1] + r15 * (nx * pulls[3] + nz * pulls[4] - ny * pulls[7])
    gz = r3 * pulls[2] + r15 * (ny * pulls[4] + nx * pulls[6]) + 3.0 * r5 * nz * pulls[5]
    radially = along - (nx * gx + ny * gy + nz * gz) * inverse
    pulls = [radially * n + g * inverse for n, g in ((nx, gx), (ny, gy), (nz, gz))]
    highs = []
    for k in range(TILES):
        blocks = jnp.concatenate([bhot[k] * p[k : k + 1] for p in pulls], axis=0)
        highs.append(jnp.concatenate(halves(blocks), axis=0))
    blocks = jnp.concatenate(highs, axis=1).astype(BF16)
    both = dot(blocks, ghot[...], NT)
    both = both[0:96] + both[96:192]
    rows = both[0:32]
    for c in range(1, 3):
        rows = rows + pltpu.roll(both[32 * c : 32 * c + 32], 32 * c, 1)
    for b in range(27):
        leaving[b] = rows[b : b + 1]
    fourth = [
        remote(3, b, leaving.at[b], returned.at[b], OFFSETS[b]) for b in OTHERS
    ]
    for copy in fourth:
        copy.start()
    sums = [jnp.sum(p, axis=0, keepdims=True) for p in pulls] + [jnp.zeros((5, 128), F32)]
    force = pick(jnp.concatenate(sums, axis=0), spread, NT)
    own_row = rows[OWN : OWN + 1]
    force = jnp.concatenate([unrolled(own_row, c) for c in range(3)] + [sums[3]], axis=0) - force
    for copy in fourth:
        copy.wait_recv()
    back = returned[OTHERS[0]]
    for b in OTHERS[1:]:
        back = back + returned[b]
    back = jnp.concatenate([unrolled(back, c) for c in range(3)] + [sums[3]], axis=0)
    force = force + pick(back, unsend, NN)
    for c in range(3):
        force_ref[0, 0, c] = force[c : c + 1, 0:ATOMS]
    for copy in first + fourth:
        copy.wait_send()
    for level in range(-1, 2):
        for ox in range(-1, 2):
            for oy in range(-1, 2):
                if (ox, oy, level) != (0, 0, 0):
                    second(ox, oy, level, mine, (0, twin, 0)).wait_send()
                    third(ox, oy, level, (0, twin, 0)).wait_send()


def per_device(
    positions,
    species,
    send_rows,
    neighbours,
    embedding,
    self_energy,
    source_weight,
    radial_in,
    radial_out,
    mix_weight,
    read_one,
    read_hidden,
    read_two,
):
    vmem = pl.BlockSpec(memory_space=pltpu.VMEM)
    energy, forces = pl.pallas_call(
        kernel,
        out_shape=(
            jax.ShapeDtypeStruct((1, 1, 1, ATOMS), F32),
            jax.ShapeDtypeStruct((1, 1, 3, 1, ATOMS), F32),
        ),
        in_specs=[pl.BlockSpec(memory_space=pltpu.HBM)] * 13,
        out_specs=(vmem, vmem),
        scratch_shapes=[
            pltpu.VMEM((1, 1, 3, 1, ATOMS), F32),
            pltpu.VMEM((1, 1, 1, ATOMS), jnp.int32),
            pltpu.VMEM((1, 1, 1, ATOMS), jnp.int32),
            pltpu.VMEM((1, 1, ATOMS, 1, SLOTS), jnp.int32),
            pltpu.VMEM(embedding.shape, F32),
            pltpu.VMEM((1, 89), F32),
            pltpu.VMEM(source_weight.shape, F32),
            pltpu.VMEM(radial_in.shape, F32),
            pltpu.VMEM(radial_out.shape, F32),
            pltpu.VMEM(mix_weight.shape, F32),
            pltpu.VMEM((1, 128), F32),
            pltpu.VMEM((16, 128), F32),
            pltpu.VMEM((1, 16), F32),
            pltpu.VMEM((16, 128), F32),
            pltpu.VMEM((128, 128), F32),
            pltpu.VMEM((136, 128), F32),
            pltpu.VMEM((1, 1, 128), F32),
            pltpu.VMEM((32, 1, 128), F32),
            pltpu.VMEM((27, 1, 128), F32),
            pltpu.VMEM((27, 1, 128), F32),
            pltpu.VMEM((ATOMS, 128), F32),
            pltpu.VMEM((3, 9, ATOMS, 128), F32),
            pltpu.VMEM((3, GROUP, 128), F32),
            pltpu.VMEM((3, 9, ATOMS, 128), F32),
            pltpu.VMEM((3, 9, ATOMS, 128), F32),
            pltpu.VMEM((3, GROUP, EDGES), BF16),
            pltpu.VMEM((128, EDGES), BF16),
            pltpu.VMEM((128, EDGES), BF16),
            pltpu.VMEM((TILES, 32, 128), F32),
            pltpu.VMEM((4, 8, 128), F32),
            pltpu.VMEM((TILES, ORDERS, 128), F32),
            pltpu.VMEM((TILES, ORDERS, 128), F32),
            pltpu.VMEM((TILES, 8, 128), F32),
            pltpu.VMEM((TILES, 8, 8, 128), F32),
            pltpu.VMEM((2, TILES, 16, 128), F32),
            pltpu.VMEM((2, 384, EDGES), F32),
            pltpu.VMEM((2, 384, EDGES), F32),
            pltpu.VMEM((2, 256, EDGES), F32),
            pltpu.VMEM((128, EDGES), F32),
            pltpu.VMEM((HIDDEN, EDGES), F32),
            pltpu.VMEM((2, 128, EDGES), F32),
            pltpu.VMEM((256, EDGES), BF16),
            pltpu.VMEM((9, 128, 128), F32),
            pltpu.VMEM((9, 128, 128), F32),
            pltpu.SemaphoreType.DMA((4, 27)),
            pltpu.SemaphoreType.DMA((4, 27)),
            pltpu.SemaphoreType.DMA((13,)),
        ],
        compiler_params=pltpu.CompilerParams(
            collective_id=0, has_side_effects=True, vmem_limit_bytes=60 * 1024 * 1024
        ),
        name="energy_and_forces",
    )(
        positions.transpose(0, 1, 3, 2, 4),
        species,
        send_rows,
        neighbours.transpose(0, 1, 4, 2, 3),
        embedding,
        self_energy[None],
        source_weight,
        radial_in,
        radial_out,
        mix_weight,
        read_one[None],
        read_hidden.T,
        read_two[None],
    )
    return -energy, -forces.transpose(0, 1, 3, 2, 4)


def solution(mesh):
    return jax.shard_map(
        per_device,
        mesh=mesh,
        in_specs=(
            P("gx", "gy", "gz", None, None),
            P("gx", "gy", "gz", None),
            P("gx", "gy", "gz", None),
            P("gx", "gy", "gz", None, None),
            P(),
            P(),
            P(),
            P(),
            P(),
            P(),
            P(),
            P(),
            P(),
        ),
        out_specs=(P("gx", "gy", "gz", None), P("gx", "gy", "gz", None, None)),
        check_vma=False,
    )
```

```python
import functools
import math

import jax
import jax.numpy as jnp
from jax import lax
from jax.experimental import pallas as pl
from jax.experimental.pallas import tpu as pltpu
from jax.sharding import PartitionSpec as P

F32 = jnp.float32
BF16 = jnp.bfloat16
HIGHEST = lax.Precision.HIGHEST
MESH = pl.DeviceIdType.MESH
CUTOFF = 6.0
BOX = (7.5, 7.5, 5.0)
ATOMS = 18
SLOTS = 56
CHANNELS = 128
HIDDEN = 64
ORDERS = 8
ROWS = 24
GROUP = 256
EDGES = 1024
TILES = 8
CHUNK = 16
OWN = 13
OFFSETS = tuple((b // 9 - 1, b // 3 % 3 - 1, b % 3 - 1) for b in range(27))
OTHERS = tuple(
    sorted(
        (b for b in range(27) if b != OWN),
        key=lambda b: -sum(abs(o) * w for o, w in zip(OFFSETS[b], (2, 1, 4))),
    )
)
NN = ((1,), (0,))
NT = ((1,), (1,))
TN = ((0,), (0,))


def dot(left, right, dims, precision=None):
    return lax.dot_general(
        left, right, (dims, ((), ())), precision=precision, preferred_element_type=F32
    )


def pick(value, selector, dims):
    high, low = halves(value)
    middle, low = halves(low)
    parts = jnp.concatenate([high, middle, low, jnp.zeros_like(low)], axis=0).astype(BF16)
    parts = dot(parts, selector.astype(BF16), dims)
    return (parts[0:8] + parts[8:16]) + parts[16:24]


def halves(value):
    high = value.astype(BF16).astype(F32)
    return high, value - high


def dot_split(left, right, dims):
    left_high, left_low = halves(left)
    right_high, right_low = halves(right)
    left_high = left_high.astype(BF16)
    right_high = right_high.astype(BF16)
    return (
        dot(left_high, right_high, dims)
        + dot(left_high, right_low.astype(BF16), dims)
        + dot(left_low.astype(BF16), right_high, dims)
    )


def parted(value, axis):
    return jnp.concatenate(halves(value), axis=axis).astype(BF16)


def apply(left, right, dims):
    both = dot(parted(left, 0), right, dims)
    both = both[0:ROWS] + both[ROWS : 2 * ROWS]
    half = both.shape[1] // 2
    return both[:, 0:half] + both[:, half:]


def iota(shape, dim):
    return lax.broadcasted_iota(jnp.int32, shape, dim)


def over(value, divisor):
    return (value * (65536 // divisor + 1)) >> 16


def lanes(index):
    return pl.ds(pl.multiple_of(index * 128, 128), 128)


def even_series(square, first):
    total = jnp.zeros_like(square)
    for n in range(7, 0, -1):
        total = (total + 1.0) * square * (-1.0 / ((2 * n + first) * (2 * n + first - 1)))
    return total + 1.0


def column(row, rows):
    return jnp.transpose(jnp.broadcast_to(row, (128, 128)))[0:rows]


def packed(values):
    row = values[0:1]
    for c in range(1, 4):
        row = row + pltpu.roll(values[c : c + 1], 32 * c, 1)
    return row


def unrolled(values, c):
    return values if c == 0 else pltpu.roll(values, 128 - 32 * c, 1)


def kernel(
    pos_hbm,
    species_hbm,
    send_hbm,
    nbr_hbm,
    emb_hbm,
    self_hbm,
    source_hbm,
    rin_hbm,
    rout_hbm,
    mix_hbm,
    read_one_hbm,
    read_hidden_hbm,
    read_two_hbm,
    energy_ref,
    force_ref,
    pos_ref,
    species_ref,
    send_ref,
    nbr_ref,
    emb_ref,
    self_ref,
    source_ref,
    rin_ref,
    rout_ref,
    mix_ref,
    read_one_ref,
    read_hidden_ref,
    read_two_ref,
    stage,
    slots,
    table_emb,
    packet,
    arrived,
    leaving,
    returned,
    mine,
    feat,
    table,
    feat_grad,
    feat_back,
    onehot,
    ghot,
    gdeep,
    bhot,
    geo,
    basis_ref,
    dbasis_ref,
    harm,
    tall,
    edge_grad,
    radial,
    slope,
    term,
    dsilu,
    later,
    source,
    source_grad,
    acc,
    expanded,
    sent,
    received,
    loaded,
):
    me = (lax.axis_index("gx"), lax.axis_index("gy"), lax.axis_index("gz"))
    extent = (3, 16, 16)

    def device(offset):
        return tuple(lax.rem(m + (o + n), n) for m, o, n in zip(me, offset, extent))

    def minus(offset):
        return tuple(-o for o in offset)

    inputs = [
        pltpu.make_async_copy(src, dst, loaded.at[i])
        for i, (src, dst) in enumerate(
            (
                (pos_hbm, pos_ref),
                (species_hbm, species_ref),
                (send_hbm, send_ref),
                (nbr_hbm, nbr_ref),
                (emb_hbm, emb_ref),
                (self_hbm, self_ref),
                (source_hbm, source_ref),
                (rin_hbm, rin_ref),
                (rout_hbm, rout_ref),
                (mix_hbm, mix_ref),
                (read_one_hbm, read_one_ref),
                (read_hidden_hbm, read_hidden_ref),
                (read_two_hbm, read_two_ref),
            )
        )
    ]
    for copy in inputs[0:3]:
        copy.start()
    barrier = pltpu.get_barrier_semaphore()
    for b in OTHERS:
        pl.semaphore_signal(barrier, inc=1, device_id=device(OFFSETS[b]), device_id_type=MESH)
    for copy in inputs[3:]:
        copy.start()

    across = jnp.where(lax.rem(me[2], 4) < 2, -1, 1)
    twin = 1 - 2 * lax.rem(me[1], 2)
    off = -twin

    def place_of(ox, oy):
        return 3 * (ox + 1) + oy + 1

    def remote(phase, index, src, dst, offset):
        return pltpu.make_async_remote_copy(
            src_ref=src,
            dst_ref=dst,
            send_sem=sent.at[phase, index],
            recv_sem=received.at[phase, index],
            device_id=device(offset),
            device_id_type=MESH,
        )

    stage[...] = jnp.zeros_like(stage)
    for copy in inputs[0:3]:
        copy.wait()
    for c in range(3):
        stage[c : c + 1, 0:ATOMS] = pos_ref[0, 0, c]
    stage[3:4, 0:ATOMS] = species_ref[0, 0].astype(F32)
    stage[8:9, 0:ATOMS] = send_ref[0, 0].astype(F32)
    lane = iota((128, 128), 1)
    row = iota((128, 128), 0)
    send_row = jnp.where(lane[0:1] < ATOMS, stage[8:9], -5.0)
    own = stage[0:8]
    to_send = (row.astype(F32) == send_row).astype(F32)
    own_send = pick(own, to_send, NN)
    packet[0] = packed(own_send)
    arrived[OWN] = packed(own)
    arrived[27:32] = jnp.zeros((5, 1, 128), F32)
    pl.semaphore_wait(barrier, 26)
    ways = [(dx, dy, level) for level in (across, -across) for dx in (-1, 1, 0) for dy in (-1, 1, 0)]
    ways += [(dx, dy, 0) for dx in (-1, 1, 0) for dy in (-1, 1, 0) if (dx, dy) != (0, 0)]

    def slot_of(way):
        return 9 * (way[0] + 1) + 3 * (way[1] + 1) + way[2] + 1

    first = [
        remote(0, slot_of(minus(w)), packet.at[0], arrived.at[slot_of(minus(w))], w) for w in ways
    ]
    for copy in first:
        copy.start()

    send_col = column(send_row, 128)
    lane_atom = jnp.where(lane < 7 * ATOMS, lane - ATOMS * over(lane, ATOMS), -7)
    select = (send_col[0:ROWS] == lane_atom[0:ROWS].astype(F32)).astype(F32)
    select_wide = jnp.concatenate([select, select], axis=1).astype(BF16)
    select_deep = jnp.concatenate([select, select], axis=0).astype(BF16)
    unsend = (send_col == lane.astype(F32)).astype(F32)
    spread = (row == lane_atom).astype(F32)
    centre = pick(own, spread, NN)

    slots[...] = jnp.zeros_like(slots)
    inputs[3].wait()
    for a in range(ATOMS):
        slots[a : a + 1, 0:SLOTS] = (nbr_ref[0, 0, a] + 1).astype(F32)
    by_slot = jnp.transpose(slots[...])
    named = by_slot[0:8]
    for j in range(1, 7):
        named = named + pltpu.roll(by_slot[8 * j : 8 * j + 8], ATOMS * j, 1)
    named = named.astype(jnp.int32) - 1
    outer = jnp.maximum(named - ATOMS, 0)
    block = jnp.where(named < 0, -1, jnp.where(named < ATOMS, OWN, over(outer, ATOMS)))
    member = jnp.where(named < ATOMS, named, outer - ATOMS * over(outer, ATOMS))
    usable = (named >= 0).astype(F32)

    table_row = iota((GROUP, 128), 0)
    table_place = over(table_row, ROWS)
    table_member = table_row - ROWS * table_place
    held = (table_member < ATOMS) & (table_place < 9)
    for q in range(3):
        label = ATOMS + ATOMS * (3 * table_place + q) + table_member
        label = jnp.where(held, label, -2)
        if q == 1:
            label = jnp.concatenate(
                [label[0 : 4 * ROWS], send_col[0:ROWS].astype(jnp.int32), label[5 * ROWS :]],
                axis=0,
            )
        for k in range(TILES):
            tile = slice(128 * k, 128 * k + 128)
            onehot[q, :, tile] = (label == named[k : k + 1]).astype(F32).astype(BF16)
    for k in range(TILES):
        tile = slice(128 * k, 128 * k + 128)
        ghot[:, tile] = (row == member[k : k + 1]).astype(F32).astype(BF16)
        bhot[k] = (row[0:32] == block[k : k + 1]).astype(F32)

    table_emb[...] = jnp.zeros_like(table_emb)
    for copy in inputs[4:]:
        copy.wait()
    table_emb[0:89] = emb_ref[...]
    table_emb[128:129, 0:89] = self_ref[...]
    embedding = table_emb[0:128]
    species_col = column(own_send[3:4], ROWS)
    own_hot = (
        (species_col == lane[0:ROWS].astype(F32)) & (row[0:ROWS] < ATOMS)
    ).astype(F32)
    h_zero = dot(own_hot, embedding, NN, HIGHEST)
    isolated = jnp.sum(own_hot * table_emb[128:129], axis=1, keepdims=True)
    emb_source = dot_split(jnp.transpose(source_ref[0]), embedding, NT)
    emb_source = parted(emb_source, 1)

    rin_high, rin_low = halves(jnp.concatenate([rin_ref[0], rin_ref[1]], axis=1))
    rin_wide = jnp.concatenate(
        [rin_high, rin_high, rin_low, jnp.zeros((104, 128), F32)], axis=0
    )
    rin_wide = jnp.transpose(rin_wide)[:, 0:32].astype(BF16)
    rout_wide = []
    for t in range(2):
        high, low = halves(rout_ref[t])
        rout_wide.append(
            jnp.transpose(jnp.concatenate([high, high, low, low], axis=0)).astype(BF16)
        )

    read_hidden = read_hidden_ref[...]
    chain = dot_split(mix_ref[0], source_ref[1], NN)
    chain_wide = parted(chain, 1)
    chain_deep = parted(chain, 0)
    read_in = parted(dot_split(mix_ref[1], read_hidden, NT), 1)
    read_out = parted(dot_split(read_hidden, mix_ref[1], NT), 1)
    zero_source = dot_split(h_zero, source_ref[1], NN)
    for k in range(TILES):
        tile = slice(128 * k, 128 * k + 128)
        repeated = jnp.where(row < 96, row - 32 * over(row, 32), -3)
        gdeep[:, tile] = (repeated == member[k : k + 1]).astype(F32).astype(BF16)

    for copy in first:
        copy.wait_recv()
    lane_part = over(lane[0:32], 32)
    domain = row[0:32]
    third = over(domain, 3)
    shift = jnp.where(
        lane_part == 0,
        (over(domain, 9) - 1).astype(F32) * BOX[0],
        jnp.where(
            lane_part == 1,
            (third - 3 * over(domain, 9) - 1).astype(F32) * BOX[1],
            jnp.where(lane_part == 2, (domain - 3 * third - 1).astype(F32) * BOX[2], 0.0),
        ),
    )
    nearby = arrived[...].reshape(32, 128) + shift
    nearby = jnp.concatenate([unrolled(nearby, c) for c in range(4)], axis=0)
    high, low = halves(jnp.where(lane < 32, nearby, 0.0))
    middle, low = halves(low)
    nearby = high + pltpu.roll(middle, 32, 1) + pltpu.roll(low, 64, 1)
    by_block = dot(nearby.astype(BF16), gdeep[...], NN)
    for k in range(TILES):
        tile = slice(128 * k, 128 * k + 128)
        for c in range(4):
            geo[c, k : k + 1, :] = jnp.sum(
                by_block[32 * c : 32 * c + 32, tile] * bhot[k], axis=0, keepdims=True
            )

    dx = geo[0] - centre[0:1]
    dy = geo[1] - centre[1:2]
    dz = geo[2] - centre[2:3]
    distance = jnp.sqrt(dx * dx + dy * dy + dz * dz + 0.25)
    inverse = 1.0 / distance
    nx = dx * inverse
    ny = dy * inverse
    nz = dz * inverse
    scaled = jnp.minimum(distance * (1.0 / CUTOFF), 1.0)
    square = scaled * scaled
    fifth = square * square * scaled
    sixth = fifth * scaled
    seventh = sixth * scaled
    envelope = 1.0 - 28.0 * sixth + 48.0 * seventh - 21.0 * seventh * scaled
    envelope_grad = (-168.0 * fifth + 336.0 * sixth - 168.0 * seventh) * (1.0 / CUTOFF)
    weight = math.sqrt(2.0 / CUTOFF) * inverse * usable
    weight_grad = weight * (envelope_grad - envelope * inverse)
    weight = weight * envelope
    angle = (scaled - 0.5) * math.pi
    sine_one = even_series(angle * angle, 0)
    cosine_one = -angle * even_series(angle * angle, 1)
    sine, cosine = sine_one, cosine_one
    sine_last, cosine_last = jnp.zeros_like(angle), jnp.ones_like(angle)
    for m in range(ORDERS):
        basis_ref[:, m, :] = weight * sine
        dbasis_ref[:, m, :] = weight_grad * sine + weight * cosine * ((m + 1) * math.pi / CUTOFF)
        sine, sine_last = 2.0 * cosine_one * sine - sine_last, sine
        cosine, cosine_last = 2.0 * cosine_one * cosine - cosine_last, cosine
    r3, r5, r15 = math.sqrt(3.0), math.sqrt(5.0), math.sqrt(15.0)
    for m, value in enumerate(
        (
            r3 * nx,
            r3 * ny,
            r3 * nz,
            r15 * nx * ny,
            r15 * ny * nz,
            0.5 * r5 * (3.0 * nz * nz - 1.0),
            r15 * nx * nz,
            0.5 * r15 * (nx * nx - ny * ny),
        )
    ):
        harm[:, m, :] = value
        for k in range(TILES):
            tall[k, m] = jnp.broadcast_to(value[k : k + 1], (8, 128))

    basis = jnp.concatenate([basis_ref[k] for k in range(TILES)], axis=1)

    def radial_in(value):
        high, low = halves(value)
        value = jnp.concatenate([high, low, high, jnp.zeros_like(high)], axis=0).astype(BF16)
        return dot(rin_wide, value, NN)

    pre = radial_in(basis)
    gate = 1.0 / (1.0 + jnp.exp(-pre))
    hidden = pre * gate
    dsilu[...] = gate * (1.0 + pre * (1.0 - gate))
    later[...] = hidden[HIDDEN : 2 * HIDDEN]

    def radial_out(t, value):
        high, low = halves(value[HIDDEN * t : HIDDEN * t + HIDDEN])
        deep = jnp.concatenate([high, low, high, low], axis=0).astype(BF16)
        return dot(rout_wide[t], deep, NN)

    def gather_sum(t):
        def chunk(ci, carry):
            c0 = pl.multiple_of(ci * CHUNK, CHUNK)
            rows = [pl.ds(pl.multiple_of(128 * q + c0, CHUNK), CHUNK) for q in range(3)]
            sums = [None] * 9
            for k in range(TILES):
                tile = slice(128 * k, 128 * k + 128)
                src = source[t, rows[0], tile]
                terms = [radial[t, rows[q], tile] * src for q in range(3)]
                term[t, rows[0], tile] = terms[1]
                term[t, rows[1], tile] = terms[2]
                terms = [value.reshape(CHUNK // 8, 8, 128) for value in terms]
                parts = [terms[0]]
                parts += [terms[1] * tall[k, m][None] for m in range(3)]
                parts += [terms[2] * tall[k, m][None] for m in range(3, 8)]
                sums = [p if s is None else s + p for s, p in zip(sums, parts)]
            for i in range(9):
                acc[i, rows[0], :] = sums[i].reshape(CHUNK, 128)
            return carry

        lax.fori_loop(0, CHANNELS // CHUNK, chunk, 0)

    def interaction(t):
        gather_sum(t)
        wide = acc[...].reshape(9 * 128, 128)
        wide = jnp.concatenate(halves(wide), axis=1).astype(BF16)
        moments = 0.25 * dot(select_wide, wide, NT)
        parts = [moments[:, 128 * i : 128 * i + 128] for i in range(9)]
        vector = parts[1] * parts[1] + parts[2] * parts[2] + parts[3] * parts[3]
        tensor = parts[4] * parts[4]
        for i in range(5, 9):
            tensor = tensor + parts[i] * parts[i]
        return jnp.concatenate([parts[0], vector, tensor], axis=1), parts

    def interaction_back(inv_grad, parts):
        grads = [0.25 * inv_grad[:, 0:128]]
        grads += [0.5 * inv_grad[:, 128:256] * parts[i] for i in range(1, 4)]
        grads += [0.5 * inv_grad[:, 256:384] * parts[i] for i in range(4, 9)]
        deep = jnp.concatenate(grads, axis=1)
        deep = jnp.concatenate(halves(deep), axis=0).astype(BF16)
        expanded[...] = dot(deep, select_deep, TN).reshape(9, 128, 128)

    def source_back():
        def tile_back(k, carry):
            tile = lanes(k)
            ys = harm[k]
            for ci in range(CHANNELS // CHUNK):
                rows = [slice(128 * q + CHUNK * ci, 128 * q + CHUNK * ci + CHUNK) for q in range(3)]
                wide = [expanded[i, rows[0], :] for i in range(9)]
                pulls = [wide[0], wide[1] * ys[0:1], wide[4] * ys[3:4]]
                for m in range(1, 3):
                    pulls[1] = pulls[1] + wide[1 + m] * ys[m : m + 1]
                for m in range(4, 8):
                    pulls[2] = pulls[2] + wide[1 + m] * ys[m : m + 1]
                rads = [radial[1, rows[q], tile] for q in range(3)]
                high, low = halves(rads[0] * pulls[0] + rads[1] * pulls[1] + rads[2] * pulls[2])
                source_grad[rows[0], tile] = high.astype(BF16)
                source_grad[rows[1], tile] = low.astype(BF16)
            return carry

        lax.fori_loop(0, TILES, tile_back, 0)

    def edge_back(t):
        def tile_back(k, carry):
            tile = lanes(k)
            ys = harm[k]
            slopes = [jnp.zeros((8, 128), F32)] * 9
            sums = [jnp.zeros((8, 128), F32)] * 8
            for ci in range(CHANNELS // CHUNK):
                rows = [slice(128 * q + CHUNK * ci, 128 * q + CHUNK * ci + CHUNK) for q in range(3)]
                src = source[t, rows[0], tile]
                steep = [slope[t, rows[q], tile] for q in range(3)]
                if t == 1:
                    steep = [value * src for value in steep]
                terms = [term[t, rows[q], tile] for q in range(2)]
                for m in range(9):
                    wide = expanded[m, rows[0], :]
                    q = 0 if m < 1 else 1 if m < 4 else 2
                    value = wide * steep[q]
                    slopes[m] = slopes[m] + (value[0:8] + value[8:16])
                    if m > 0:
                        value = wide * terms[q - 1]
                        sums[m - 1] = sums[m - 1] + (value[0:8] + value[8:16])
            along = slopes[0]
            for m in range(8):
                along = along + slopes[1 + m] * ys[m : m + 1]
            tops = [jnp.sum(s, axis=0, keepdims=True) for s in sums + [along]]
            tops.append(jnp.zeros((7, 128), F32))
            edge_grad[t, k] = jnp.concatenate(tops, axis=0)
            return carry

        lax.fori_loop(0, TILES, tile_back, 0)

    radial[0] = radial_out(0, hidden)
    element = geo[3]
    number = row.astype(F32)
    hots = [(number == element[k : k + 1]).astype(F32) for k in range(TILES)]
    hots = jnp.concatenate(hots, axis=1).astype(BF16)
    source[0] = dot(emb_source, jnp.concatenate([hots, hots], axis=0), NN)
    invariants, parts_one = interaction(0)

    mine[...] = (zero_source + apply(invariants, chain_wide, NN))[0:ATOMS]

    def second(ox, oy, level, src, offset):
        place = place_of(ox, oy)
        return remote(1, 9 * (1 + level) + place, src, feat.at[1 + level, place], offset)

    def outward(dx, dy, level):
        return second(-dx, -dy, -level, mine, (dx, dy, level))

    def arrival(ox, oy, level):
        return second(ox, oy, level, mine, (0, twin, 0))

    def hand_on(ox, level):
        return second(ox, off, level, feat.at[1 + level, place_of(ox, 0)], (0, twin, 0))

    for level in (across, -across):
        for dx in (-1, 1, 0):
            outward(dx, 0, level).start()
        for dx in (-1, 1, 0):
            outward(dx, off, level).start()
    outward(0, twin, 0).start()
    for dx in (-1, 1):
        outward(dx, 0, 0).start()
    for dx in (-1, 1, 0):
        outward(dx, off, 0).start()
    table[...] = jnp.zeros_like(table)
    table[1, 4 * ROWS : 4 * ROWS + ATOMS] = mine[...]
    h_one = h_zero + dot_split(invariants, mix_ref[0], NN)
    read_one = dot_split(h_one, read_hidden, NT)
    later_hidden = jnp.concatenate([later[...], later[...]], axis=0)
    radial[1] = radial_out(1, later_hidden)
    tilted = dsilu[...] * radial_in(jnp.concatenate([dbasis_ref[k] for k in range(TILES)], axis=1))
    steep = radial_out(0, tilted)
    for q in range(3):
        slope[0, 128 * q : 128 * q + 128] = steep[128 * q : 128 * q + 128] * source[0]
    slope[1] = radial_out(1, tilted)

    def relay(level, sides):
        for ox in sides:
            arrival(ox, 0, level).wait_recv()
            hand_on(ox, level).start()

    def gather(level):
        for ox in range(-1, 2):
            arrival(ox, off, level).wait_recv()
            arrival(ox, twin, level).wait_recv()
        for place in range(9):
            if not (place == 4 and isinstance(level, int)):
                table[1 + level, ROWS * place : ROWS * place + ATOMS] = feat[1 + level, place]
        turned = parted(jnp.transpose(table[1 + level]), 0)
        both = dot(turned, onehot[1 + level], NN)
        return both[0:128] + both[128:256]

    relay(0, (-1, 1))
    relay(-across, range(-1, 2))
    source[1] = gather(0)
    relay(across, range(-1, 2))
    source[1] = source[1] + gather(-across)
    source[1] = source[1] + gather(across)

    invariants, parts_two = interaction(1)
    inner = read_one + apply(invariants, read_in, NN)
    gate = 1.0 / (1.0 + jnp.exp(-inner))
    inner_grad = gate * (1.0 + inner * (1.0 - gate)) * read_two_ref[...]
    interaction_back(apply(inner_grad, read_out, NN), parts_two)
    source_back()

    def third(ox, oy, level, offset):
        place = place_of(ox, oy)
        slot = 9 * (1 + level) + place
        return remote(2, slot, feat_grad.at[1 + level, place], feat_back.at[1 + level, place], offset)

    def scatter(level):
        both = dot(onehot[1 + level], source_grad[...], NT)
        both = both[:, 0:128] + both[:, 128:256]
        for place in range(9):
            feat_grad[1 + level, place] = both[ROWS * place : ROWS * place + ATOMS]
        for ox in (-1, 1, 0):
            third(ox, twin, level, (0, twin, 0)).start()
        for ox in (-1, 1, 0):
            third(ox, off, level, (ox, off, level)).start()

    def combine(level, sides):
        for ox in sides:
            third(ox, off, level, (0, twin, 0)).wait_recv()
            place = place_of(ox, 0)
            feat_grad[1 + level, place] = (
                feat_grad[1 + level, place] + feat_back[1 + level, place_of(ox, off)]
            )
            third(ox, 0, level, (ox, 0, level)).start()

    scatter(across)
    scatter(-across)
    combine(across, (-1, 1, 0))
    scatter(0)
    combine(-across, (-1, 1, 0))
    combine(0, (-1, 1))
    grad_two = dot_split(inner_grad, read_hidden, NN) + read_one_ref[...]
    grad_two = dot_split(grad_two, mix_ref[0], NT)
    edge_back(1)
    learned = jnp.sum(h_one * read_one_ref[...], axis=1, keepdims=True) + jnp.sum(
        inner * gate * read_two_ref[...], axis=1, keepdims=True
    )
    energy = jnp.sum((isolated + learned) * unsend[0:ROWS], axis=0, keepdims=True)
    energy_ref[0, 0] = -energy[:, 0:ATOMS]
    third(0, off, 0, (0, twin, 0)).wait_recv()
    total = feat_grad[1, 4] + feat_back[1, place_of(0, off)]
    for level in (0, across, -across):
        for ox in range(-1, 2):
            if not (ox == 0 and isinstance(level, int)):
                third(ox, 0, level, (0, twin, 0)).wait_recv()
                total = total + feat_back[1 + level, place_of(ox, 0)]
            third(ox, twin, level, (0, twin, 0)).wait_recv()
            total = total + feat_back[1 + level, place_of(ox, twin)]
    own_rows = slice(4 * ROWS, 4 * ROWS + ROWS)
    table[1, 4 * ROWS : 4 * ROWS + ATOMS] = total
    grad_one = grad_two + apply(table[1, own_rows], chain_deep, NT)

    interaction_back(grad_one, parts_one)
    edge_back(0)

    pulls = [edge_grad[0, :, m, :] + edge_grad[1, :, m, :] for m in range(9)]
    along = pulls[8]
    gx = r3 * pulls[0] + r15 * (ny * pulls[3] + nz * pulls[6] + nx * pulls[7])
    gy = r3 * pulls[1] + r15 * (nx * pulls[3] + nz * pulls[4] - ny * pulls[7])
    gz = r3 * pulls[2] + r15 * (ny * pulls[4] + nx * pulls[6]) + 3.0 * r5 * nz * pulls[5]
    radially = along - (nx * gx + ny * gy + nz * gz) * inverse
    pulls = [radially * n + g * inverse for n, g in ((nx, gx), (ny, gy), (nz, gz))]
    highs = []
    for k in range(TILES):
        blocks = jnp.concatenate([bhot[k] * p[k : k + 1] for p in pulls], axis=0)
        highs.append(jnp.concatenate(halves(blocks), axis=0))
    blocks = jnp.concatenate(highs, axis=1).astype(BF16)
    both = dot(blocks, ghot[...], NT)
    both = both[0:96] + both[96:192]
    rows = both[0:32]
    for c in range(1, 3):
        rows = rows + pltpu.roll(both[32 * c : 32 * c + 32], 32 * c, 1)
    for b in range(27):
        leaving[b] = rows[b : b + 1]
    fourth = [
        remote(3, slot_of(w), leaving.at[slot_of(w)], returned.at[slot_of(w)], w) for w in ways
    ]
    for copy in fourth:
        copy.start()
    sums = [jnp.sum(p, axis=0, keepdims=True) for p in pulls] + [jnp.zeros((5, 128), F32)]
    force = pick(jnp.concatenate(sums, axis=0), spread, NT)
    own_row = rows[OWN : OWN + 1]
    force = jnp.concatenate([unrolled(own_row, c) for c in range(3)] + [sums[3]], axis=0) - force
    for copy in fourth:
        copy.wait_recv()
    back = returned[OTHERS[0]]
    for b in OTHERS[1:]:
        back = back + returned[b]
    back = jnp.concatenate([unrolled(back, c) for c in range(3)] + [sums[3]], axis=0)
    force = force + pick(back, unsend, NN)
    for c in range(3):
        force_ref[0, 0, c] = force[c : c + 1, 0:ATOMS]
    for copy in first + fourth:
        copy.wait_send()
    for level in range(-1, 2):
        for ox in range(-1, 2):
            for oy in range(-1, 2):
                if (ox, oy, level) != (0, 0, 0):
                    second(ox, oy, level, mine, (0, twin, 0)).wait_send()
                    third(ox, oy, level, (0, twin, 0)).wait_send()


def per_device(
    positions,
    species,
    send_rows,
    neighbours,
    embedding,
    self_energy,
    source_weight,
    radial_in,
    radial_out,
    mix_weight,
    read_one,
    read_hidden,
    read_two,
):
    vmem = pl.BlockSpec(memory_space=pltpu.VMEM)
    energy, forces = pl.pallas_call(
        kernel,
        out_shape=(
            jax.ShapeDtypeStruct((1, 1, 1, ATOMS), F32),
            jax.ShapeDtypeStruct((1, 1, 3, 1, ATOMS), F32),
        ),
        in_specs=[pl.BlockSpec(memory_space=pltpu.HBM)] * 13,
        out_specs=(vmem, vmem),
        scratch_shapes=[
            pltpu.VMEM((1, 1, 3, 1, ATOMS), F32),
            pltpu.VMEM((1, 1, 1, ATOMS), jnp.int32),
            pltpu.VMEM((1, 1, 1, ATOMS), jnp.int32),
            pltpu.VMEM((1, 1, ATOMS, 1, SLOTS), jnp.int32),
            pltpu.VMEM(embedding.shape, F32),
            pltpu.VMEM((1, 89), F32),
            pltpu.VMEM(source_weight.shape, F32),
            pltpu.VMEM(radial_in.shape, F32),
            pltpu.VMEM(radial_out.shape, F32),
            pltpu.VMEM(mix_weight.shape, F32),
            pltpu.VMEM((1, 128), F32),
            pltpu.VMEM((16, 128), F32),
            pltpu.VMEM((1, 16), F32),
            pltpu.VMEM((16, 128), F32),
            pltpu.VMEM((128, 128), F32),
            pltpu.VMEM((136, 128), F32),
            pltpu.VMEM((1, 1, 128), F32),
            pltpu.VMEM((32, 1, 128), F32),
            pltpu.VMEM((27, 1, 128), F32),
            pltpu.VMEM((27, 1, 128), F32),
            pltpu.VMEM((ATOMS, 128), F32),
            pltpu.VMEM((3, 9, ATOMS, 128), F32),
            pltpu.VMEM((3, GROUP, 128), F32),
            pltpu.VMEM((3, 9, ATOMS, 128), F32),
            pltpu.VMEM((3, 9, ATOMS, 128), F32),
            pltpu.VMEM((3, GROUP, EDGES), BF16),
            pltpu.VMEM((128, EDGES), BF16),
            pltpu.VMEM((128, EDGES), BF16),
            pltpu.VMEM((TILES, 32, 128), F32),
            pltpu.VMEM((4, 8, 128), F32),
            pltpu.VMEM((TILES, ORDERS, 128), F32),
            pltpu.VMEM((TILES, ORDERS, 128), F32),
            pltpu.VMEM((TILES, 8, 128), F32),
            pltpu.VMEM((TILES, 8, 8, 128), F32),
            pltpu.VMEM((2, TILES, 16, 128), F32),
            pltpu.VMEM((2, 384, EDGES), F32),
            pltpu.VMEM((2, 384, EDGES), F32),
            pltpu.VMEM((2, 256, EDGES), F32),
            pltpu.VMEM((128, EDGES), F32),
            pltpu.VMEM((HIDDEN, EDGES), F32),
            pltpu.VMEM((2, 128, EDGES), F32),
            pltpu.VMEM((256, EDGES), BF16),
            pltpu.VMEM((9, 128, 128), F32),
            pltpu.VMEM((9, 128, 128), F32),
            pltpu.SemaphoreType.DMA((4, 27)),
            pltpu.SemaphoreType.DMA((4, 27)),
            pltpu.SemaphoreType.DMA((13,)),
        ],
        compiler_params=pltpu.CompilerParams(
            collective_id=0, has_side_effects=True, vmem_limit_bytes=60 * 1024 * 1024
        ),
        name="energy_and_forces",
    )(
        positions.transpose(0, 1, 3, 2, 4),
        species,
        send_rows,
        neighbours.transpose(0, 1, 4, 2, 3),
        embedding,
        self_energy[None],
        source_weight,
        radial_in,
        radial_out,
        mix_weight,
        read_one[None],
        read_hidden.T,
        read_two[None],
    )
    return -energy, -forces.transpose(0, 1, 3, 2, 4)


def solution(mesh):
    return jax.shard_map(
        per_device,
        mesh=mesh,
        in_specs=(
            P("gx", "gy", "gz", None, None),
            P("gx", "gy", "gz", None),
            P("gx", "gy", "gz", None),
            P("gx", "gy", "gz", None, None),
            P(),
            P(),
            P(),
            P(),
            P(),
            P(),
            P(),
            P(),
            P(),
        ),
        out_specs=(P("gx", "gy", "gz", None), P("gx", "gy", "gz", None, None)),
        check_vma=False,
    )
```
